128 devices in a mesh: row: 8 (over z, x_hi), col: 16 (over y, x_lo, core).
Axes of the slice: x: 4 (x_hi: 2, x_lo: 2; x = x_hi * 2 + x_lo), y: 4, z: 4, core: 2. Of those that a mesh axis runs over, the one named last changes fastest.
Arguments:
- object_now: float32 [2, 2048, 8192], P(None, 'row', 'col'), may hold values from -5 to 5
- object_prev: float32 [2, 2048, 8192], P(None, 'row', 'col'), may hold values from -5 to 5
- probe: float32 [2, 256, 256], replicated, may hold values from -4 to 4
- amplitudes: float32 [8, 16, 4, 256, 256], P('row', 'col'), may hold values from 0.2 to 3
- pos_row: int32 [8, 16, 4], P('row', 'col'), may hold values from 0 to 255
- pos_col: int32 [8, 16, 4], P('row', 'col'), may hold values from 0 to 511
- counts: int32 [8, 16], P('row', 'col'), may hold values from 1 to 4, as said below
Outputs:
- object_new: float32 [2, 2048, 8192], P(None, 'row', 'col')
- probe_new: float32 [2, 256, 256], replicated
The draws below stay inside these ranges and needn't reach their ends.
Inputs may be any that keep to these rules, and one draw needn't show every extreme that they name: Tile (r, c) uses its first counts[r, c] slots; some tile uses all 4.
All inputs are finite; a program needn't handle non-finite values.
Results may differ from the reference program's by a relative error of at most 0.0003.
Values sent between devices are 32-bit elements; how exact they have to be, the bound alone decides.
No kernel may reach another device: no remote copies, remote signals or barrier semaphores. Data moves between devices by JAX's collectives and lax.ppermute only.
A program may use at most 384 MiB of HBM per device.

```python
import math
import jax
import jax.numpy as jnp
from jax import lax

PATCH = 256
TR = 256
TC = 512
PMAX = 4
LEVELS = 4
NR = 2048
NC = 8192
N_ROW = 8
N_COL = 16


def draw_counts(key, part):
    key = jax.random.fold_in(key, 7)
    key_low, key_high, key_pick, key_spot = jax.random.split(key, 4)
    lighter = jax.random.randint(key_low, (N_ROW * N_COL,), 1, PMAX // 2 + 1)
    heavier = jax.random.randint(key_high, (N_ROW * N_COL,), PMAX // 2, PMAX + 1)
    picked = jax.random.randint(key_pick, (N_ROW * N_COL,), 0, 4) == 0
    loads = jnp.where(picked, heavier, lighter)
    spot_index = jax.random.randint(key_spot, (), 0, N_ROW * N_COL)
    loads = loads.at[spot_index].set(PMAX)
    return loads.reshape(N_ROW, N_COL).astype(jnp.int32)


def plant(values, rng, smallest, largest):
    dims = values.shape
    index_at = [jax.random.randint(jax.random.fold_in(rng, axis), (), 0, dims[axis]) for axis in range(len(dims))]
    values = values.at[tuple(index_at)].set(smallest)
    longest = dims.index(max(dims))
    index_at[longest] = (index_at[longest] + 1) % dims[longest]
    return values.at[tuple(index_at)].set(largest)


def steps_of(key, shape, pieces, least, top_value):
    def one(position, blocks):
        steps = jax.random.uniform(jax.random.fold_in(jax.random.fold_in(key, 6), position), (blocks,), jnp.float32, least / len(pieces), top_value / len(pieces))
        return jnp.repeat(jnp.exp(steps), shape[position] // blocks).reshape((-1,) + (1,) * (len(shape) - position - 1))

    gain = one(*pieces[0])
    for cut in pieces[1:]:
        gain = gain * one(*cut)
    return gain


def gaussian(key, extent, width, bound, cuts=(), kind=jnp.bfloat16):
    values = width * jax.random.normal(key, extent, jnp.float32)
    if cuts:
        values = values * steps_of(key, extent, cuts, -0.22, 0.18)
    return jnp.clip(values, -bound, bound).astype(kind)


def setup_inputs(seed: int = 0) -> dict:
    key_of = jax.random.split(jax.random.key(seed), 8)
    object_now = gaussian(key_of[0], (2, NR, NC), 0.7, 5.0, ((1, 8), (2, 16)), jnp.float32)
    object_prev = gaussian(key_of[1], (2, NR, NC), 0.7, 5.0, ((1, 8), (2, 16)), jnp.float32)
    probe = gaussian(key_of[2], (2, PATCH, PATCH), 0.5, 4.0, (), jnp.float32)
    amplitudes = jnp.clip(jnp.exp(math.log(3.0) - 2.7080502 * jax.random.uniform(key_of[3], (N_ROW, N_COL, PMAX, PATCH, PATCH), jnp.float32) ** steps_of(key_of[3], (N_ROW, N_COL, PMAX, PATCH, PATCH), ((0, 8), (1, 16)), -0.2, 0.2)), 0.2, 3.0)
    pos_row = plant(jax.random.randint(key_of[4], (N_ROW, N_COL, PMAX), 0, TR), jax.random.fold_in(key_of[4], 1), 0, TR - 1).astype(jnp.int32)
    pos_col = plant(jax.random.randint(key_of[5], (N_ROW, N_COL, PMAX), 0, TC), jax.random.fold_in(key_of[5], 1), 0, TC - 1).astype(jnp.int32)
    counts = draw_counts(jax.random.fold_in(key_of[7], 71), 0)
    return {"object_now": object_now, "object_prev": object_prev, "probe": probe, "amplitudes": amplitudes, "pos_row": pos_row, "pos_col": pos_col, "counts": counts}


MOMENTUM = 0.6
STEP_OBJECT = 0.5
PROBE_STEP = 2.0
THRESHOLD = 0.3
FLOOR = 0.5

def dft_tables(length):
    points = jnp.arange(length, dtype=jnp.int32)
    phase_index = points[:, None] * points[None, :] % length
    angles = phase_index.astype(jnp.float32) * (-2.0 * math.pi / length)
    factor = 1.0 / math.sqrt(length)
    return (jnp.cos(angles) * factor, jnp.sin(angles) * factor)

def left_product(table, values):
    return jnp.einsum('jk,bkl->bjl', table, values, precision=lax.Precision.HIGHEST)

def right_product(values, table):
    return jnp.einsum('bjl,lm->bjm', values, table, precision=lax.Precision.HIGHEST)

def transform(real_part, imag_part, table_real, table_imag):
    left_real = left_product(table_real, real_part) - left_product(table_imag, imag_part)
    left_imag = left_product(table_real, imag_part) + left_product(table_imag, real_part)
    out_real = right_product(left_real, table_real) - right_product(left_imag, table_imag)
    out_imag = right_product(left_real, table_imag) + right_product(left_imag, table_real)
    return (out_real, out_imag)

def patch_gradients(windows, probe, amplitude, live_mask, table_real, table_imag):
    window_real = windows[:, 0]
    window_imag = windows[:, 1]
    probe_real = probe[0]
    probe_imag = probe[1]
    exit_real = probe_real * window_real - probe_imag * window_imag
    exit_imag = probe_real * window_imag + probe_imag * window_real
    far_real, far_imag = transform(exit_real, exit_imag, table_real, table_imag)
    modulus = jnp.sqrt(far_real * far_real + far_imag * far_imag)
    remain = 1.0 - amplitude / jnp.maximum(modulus, FLOOR)
    back_real, back_imag = transform(far_real * remain, far_imag * remain, table_real, -table_imag)
    weight = live_mask[:, None, None]
    back_real = back_real * weight
    back_imag = back_imag * weight
    object_real = probe_real * back_real + probe_imag * back_imag
    object_imag = probe_real * back_imag - probe_imag * back_real
    probe_real_term = lax.optimization_barrier(jnp.sum(window_real * back_real + window_imag * back_imag, axis=0))
    probe_imag_term = lax.optimization_barrier(jnp.sum(window_real * back_imag - window_imag * back_real, axis=0))
    return (jnp.stack([object_real, object_imag], axis=1), jnp.stack([probe_real_term, probe_imag_term]))

def scatter_patches(gradient, terms, starts_row, starts_col):

    def add_patch(slot_index, running):
        corner = (jnp.int32(0), starts_row[slot_index], starts_col[slot_index])
        current = lax.dynamic_slice(running, corner, terms.shape[1:])
        return lax.dynamic_update_slice(running, current + terms[slot_index], corner)
    return lax.fori_loop(0, terms.shape[0], add_patch, gradient)

def shrink(detail):
    magnitude = jnp.sqrt(detail[0] * detail[0] + detail[1] * detail[1])
    factor = jnp.maximum(magnitude - THRESHOLD, 0.0) / jnp.maximum(magnitude, THRESHOLD)
    return detail * factor[None]

def haar_shrink(field, depth_left):
    if depth_left == 0:
        return field
    height = field.shape[1] // 2
    breadth = field.shape[2] // 2
    blocks = field.reshape(2, height, 2, breadth, 2)
    north_west = blocks[:, :, 0, :, 0]
    north_east = blocks[:, :, 0, :, 1]
    south_west = blocks[:, :, 1, :, 0]
    south_east = blocks[:, :, 1, :, 1]
    coarse = (north_west + north_east + south_west + south_east) * 0.5
    across = shrink((north_west - north_east + south_west - south_east) * 0.5)
    downward = shrink((north_west + north_east - south_west - south_east) * 0.5)
    diagonal = shrink((north_west - north_east - south_west + south_east) * 0.5)
    coarse = haar_shrink(coarse, depth_left - 1)
    corner_one = (coarse + across + downward + diagonal) * 0.5
    corner_two = (coarse - across + downward - diagonal) * 0.5
    corner_three = (coarse + across - downward - diagonal) * 0.5
    corner_four = (coarse - across - downward + diagonal) * 0.5
    upper_pair = jnp.stack([corner_one, corner_two], axis=-1)
    lower_pair = jnp.stack([corner_three, corner_four], axis=-1)
    return jnp.stack([upper_pair, lower_pair], axis=2).reshape(2, 2 * height, 2 * breadth)

def reference(object_now, object_prev, probe, amplitudes, pos_row, pos_col, counts):
    momentum_point = object_now + MOMENTUM * (object_now - object_prev)
    margin = PATCH // 2
    padded = jnp.pad(momentum_point, ((0, 0), (margin, margin), (margin, margin)))
    table_real, table_imag = dft_tables(PATCH)
    slot_ids = jnp.arange(PMAX, dtype=jnp.int32)

    def one_tile(state_pair, tile_id):
        gradient, probe_sum = state_pair
        tile_row = tile_id // N_COL
        tile_col = tile_id % N_COL
        starts_row = (tile_row * TR + pos_row[tile_row, tile_col]).astype(jnp.int32)
        starts_col = (tile_col * TC + pos_col[tile_row, tile_col]).astype(jnp.int32)
        windows = jax.vmap(lambda row_start, col_start: lax.dynamic_slice(padded, (jnp.int32(0), row_start, col_start), (2, PATCH, PATCH)))(starts_row, starts_col)
        live_mask = (slot_ids < counts[tile_row, tile_col]).astype(jnp.float32)
        object_terms, probe_terms = patch_gradients(windows, probe, amplitudes[tile_row, tile_col], live_mask, table_real, table_imag)
        gradient = scatter_patches(gradient, object_terms, starts_row, starts_col)
        return ((gradient, probe_sum + probe_terms), None)
    initial = (jnp.zeros_like(padded), jnp.zeros_like(probe))
    (gradient, probe_sum), unused = lax.scan(one_tile, initial, jnp.arange(N_ROW * N_COL, dtype=jnp.int32))
    interior = gradient[:, margin:margin + NR, margin:margin + NC]
    object_new = haar_shrink(momentum_point - STEP_OBJECT * interior, LEVELS)
    probe_new = probe - PROBE_STEP / (PMAX * N_ROW * N_COL) * probe_sum
    return (object_new, probe_new)
```

```python
import math

import jax
import jax.numpy as jnp
import ml_dtypes
import numpy as np
from jax import lax
from jax.experimental import pallas as pl
from jax.experimental.pallas import tpu as pltpu
from jax.sharding import PartitionSpec as P

LEVELS = 4
MOMENTUM = 0.6
STEP_OBJECT = 0.5
PROBE_STEP = 2.0
THRESHOLD = 0.3
FLOOR = 0.5

AXES = ("row", "pair", "core")
CHIPS = ("row", "pair")
LANES = 128
TILE = 8
VMEM_LIMIT = 28 * 1024 * 1024


def split_table(table):
    high = table.astype(ml_dtypes.bfloat16)
    low = (table - high.astype(np.float64)).astype(ml_dtypes.bfloat16)
    return high, low


def dft_tables(length):
    half = length // 2
    points = np.arange(half)
    angles = (points[:, None] * points[None, :] % half) * (-2.0 * math.pi / half)
    real = np.cos(angles) / math.sqrt(length)
    imag = np.sin(angles) / math.sqrt(length)
    left_high, left_low = split_table(np.block([[real, -imag], [imag, real]]))
    right_high, right_low = split_table(np.block([[real, imag], [-imag, real]]))
    turn = points * (-2.0 * math.pi / length)
    twiddle = np.stack([np.cos(turn), np.sin(turn)]).astype(np.float32)
    return (
        np.concatenate([left_high, left_high, left_low], axis=1),
        np.concatenate([right_high, right_high, right_low], axis=0),
        np.repeat(twiddle[:, :, None], LANES, axis=2),
        np.repeat(twiddle[:, None, :], half, axis=1),
    )


def split_value(value):
    high = value.astype(jnp.bfloat16)
    low = (value - high.astype(jnp.float32)).astype(jnp.bfloat16)
    return high, low


def times(real, imag, twiddle):
    cosine, sine = twiddle
    return real * cosine - imag * sine, real * sine + imag * cosine


def left_product(blocks, table):
    half = blocks[0][0].shape[0]
    width = blocks[0][0].shape[1]
    value = jnp.concatenate(
        [jnp.concatenate([real, imag], axis=0) for real, imag in blocks], axis=1
    )
    high, low = split_value(value)
    out = jnp.dot(
        table[...],
        jnp.concatenate([high, low, high], axis=0),
        preferred_element_type=jnp.float32,
    )
    return [
        (out[:half, index * width : (index + 1) * width], out[half:, index * width : (index + 1) * width])
        for index in range(len(blocks))
    ]


def right_product(blocks, table):
    half = blocks[0][0].shape[1]
    value = jnp.concatenate(
        [jnp.concatenate([real, imag], axis=1) for real, imag in blocks], axis=0
    )
    high, low = split_value(value)
    out = jnp.dot(
        jnp.concatenate([high, low, high], axis=1),
        table[...],
        preferred_element_type=jnp.float32,
    )
    return [
        (out[index * half : (index + 1) * half, :half], out[index * half : (index + 1) * half, half:])
        for index in range(len(blocks))
    ]


def forward(real, imag, left_table, right_table, row_twiddle, lane_twiddle):
    half = real.shape[0] // 2
    wide_twiddle = [jnp.concatenate([part, part], axis=1) for part in row_twiddle]
    total = (real[:half] + real[half:], imag[:half] + imag[half:])
    gap = times(real[:half] - real[half:], imag[:half] - imag[half:], wide_twiddle)
    blocks = []
    for real, imag in left_product([total, gap], left_table):
        blocks.append((real[:, :half] + real[:, half:], imag[:, :half] + imag[:, half:]))
        blocks.append(
            times(real[:, :half] - real[:, half:], imag[:, :half] - imag[:, half:], lane_twiddle)
        )
    return right_product(blocks, right_table)


def backward(blocks, left_table, right_table, row_twiddle, lane_twiddle):
    blocks = right_product(blocks, right_table)
    wide_twiddle = [jnp.concatenate([part, part], axis=1) for part in row_twiddle]
    joined = []
    for parity in range(2):
        even_real, even_imag = blocks[2 * parity]
        odd_real, odd_imag = times(*blocks[2 * parity + 1], lane_twiddle)
        joined.append(
            (
                jnp.concatenate([even_real + odd_real, even_real - odd_real], axis=1),
                jnp.concatenate([even_imag + odd_imag, even_imag - odd_imag], axis=1),
            )
        )
    (even_real, even_imag), odd = left_product(joined, left_table)
    odd_real, odd_imag = times(*odd, wide_twiddle)
    return (
        jnp.concatenate([even_real + odd_real, even_real - odd_real], axis=0),
        jnp.concatenate([even_imag + odd_imag, even_imag - odd_imag], axis=0),
    )


def amplitude_kernel(amplitude, table, out, sorted_lanes):
    slots, size, _ = amplitude.shape
    half = size // 2
    for slot in range(slots):
        value = amplitude[slot]
        high = value.astype(jnp.bfloat16)
        rest = value - high.astype(jnp.float32)
        middle, low = split_value(rest)
        ordered = jnp.dot(
            jnp.concatenate([high, middle, low], axis=1),
            table[...],
            preferred_element_type=jnp.float32,
        )
        for index in range(2):
            sorted_lanes[slot, index] = ordered[:, index * half : (index + 1) * half]
            for parity in range(2):
                out[slot, 2 * parity + index] = sorted_lanes[slot, index, pl.ds(parity, half, stride=2), :]


def ordered_amplitude(amplitude):
    slots, size, _ = amplitude.shape
    half = size // 2
    table = np.zeros((size, size), np.float32)
    table[2 * np.arange(half), np.arange(half)] = 1
    table[2 * np.arange(half) + 1, half + np.arange(half)] = 1
    table = np.concatenate([table] * 3, axis=0).astype(ml_dtypes.bfloat16)
    vmem = pl.BlockSpec(memory_space=pltpu.VMEM)
    return pl.pallas_call(
        amplitude_kernel,
        out_shape=pltpu.VMEM((slots, 4, half, half), jnp.float32),
        in_specs=[vmem, vmem],
        out_specs=vmem,
        scratch_shapes=[pltpu.VMEM((slots, 2, size, half), jnp.float32)],
        compiler_params=pltpu.CompilerParams(vmem_limit_bytes=VMEM_LIMIT),
        cost_estimate=pl.CostEstimate(
            flops=2 * slots * size**3 * 3, bytes_accessed=8 * slots * size**2, transcendentals=0
        ),
        name="ordered_amplitude",
    )(amplitude, jnp.asarray(table))


def patch_kernel(
    counts,
    rows,
    cols,
    core,
    centre,
    top,
    bottom,
    near_mid,
    far_mid,
    near_corner,
    far_top,
    far_bottom,
    probe,
    amplitude,
    left_table,
    right_table,
    row_table,
    lane_table,
    inner_out,
    up_out,
    down_out,
    near_mid_out,
    far_mid_out,
    given_out,
    far_top_out,
    far_bottom_out,
    probe_out,
    extended,
    gradient,
    probe_sum,
    sems,
):
    size = probe.shape[1]
    margin = size // 2
    height, width = centre.shape[1:]
    inner = pl.ds(margin, width)
    near = pl.ds(pl.multiple_of((1 - core[0]) * (margin + width), LANES), margin)
    far = pl.ds(pl.multiple_of(core[0] * (margin + width), LANES), margin)
    head, middle, tail = pl.ds(0, margin), pl.ds(margin, height), pl.ds(margin + height, margin)
    moves = [
        (centre, extended.at[:, middle, inner]),
        (near_mid, extended.at[:, middle, near]),
        (far_mid, extended.at[:, middle, far]),
        (top, extended.at[:, head, inner]),
        (bottom, extended.at[:, tail, inner]),
        (far_top, extended.at[:, head, far]),
        (far_bottom, extended.at[:, tail, far]),
        (near_corner.at[:, head, :], extended.at[:, head, near]),
        (near_corner.at[:, pl.ds(margin, margin), :], extended.at[:, tail, near]),
    ]
    copies = [
        pltpu.make_async_copy(source, target, sems.at[index])
        for index, (source, target) in enumerate(moves)
    ]
    for copy in copies:
        copy.start()
    gradient[...] = jnp.zeros_like(gradient)
    probe_sum[...] = jnp.zeros_like(probe_sum)
    for copy in copies:
        copy.wait()
    tile = (1, TILE, LANES)
    lane = lax.broadcasted_iota(jnp.int32, tile, 2)
    sublane = lax.broadcasted_iota(jnp.int32, tile, 1)
    tiles = size // TILE
    pieces = size // LANES

    tables = (
        left_table,
        right_table,
        (row_table[0], row_table[1]),
        (lane_table[0], lane_table[1]),
    )

    def place(slot):
        row_shift = lax.rem(rows[slot], TILE)
        col_shift = lax.rem(cols[slot], LANES)
        row = pl.multiple_of(rows[slot] - row_shift, TILE)
        col = pl.multiple_of(cols[slot] - col_shift, LANES)
        areas = [
            (pl.ds(row, size + TILE), pl.ds(col + LANES * piece, LANES))
            for piece in range(pieces + 1)
        ]
        return row_shift, col_shift, areas

    def window(part, row_shift, col_shift, areas):
        columns = [
            pltpu.roll(
                extended[(part,) + area].reshape(tiles + 1, TILE, LANES),
                lax.rem(LANES - col_shift, LANES),
                2,
            )
            for area in areas
        ]
        result = []
        for piece in range(pieces):
            value = jnp.where(lane < LANES - col_shift, columns[piece], columns[piece + 1])
            value = pltpu.roll(value, lax.rem(TILE - row_shift, TILE), 1)
            value = jnp.where(sublane < TILE - row_shift, value[:tiles], value[1:])
            result.append(value.reshape(size, LANES))
        return jnp.concatenate(result, axis=1)

    def add_term(part, term, row_shift, col_shift, areas):
        columns = []
        ended = jnp.zeros(tile, jnp.float32)
        for piece in range(pieces):
            value = term[:, LANES * piece : LANES * (piece + 1)].reshape(tiles, TILE, LANES)
            value = pltpu.roll(value, row_shift, 1)
            value = jnp.where(
                sublane >= row_shift,
                jnp.concatenate([value, ended], axis=0),
                jnp.concatenate([ended, value], axis=0),
            )
            columns.append(pltpu.roll(value, col_shift, 2))
        ended = jnp.zeros_like(columns[0])
        columns = [ended] + columns + [ended]
        for piece, area in enumerate(areas):
            block = jnp.where(lane >= col_shift, columns[piece + 1], columns[piece])
            gradient[(part,) + area] += block.reshape(size + TILE, LANES)

    def some_patches(slots):
        places = [place(slot) for slot in slots]
        windows = [[window(part, *where) for part in range(2)] for where in places]
        probe_real = probe[0]
        probe_imag = probe[1]
        far_fields = [
            forward(
                probe_real * real - probe_imag * imag, probe_real * imag + probe_imag * real, *tables
            )
            for real, imag in windows
        ]
        residuals = []
        for slot, far_field in zip(slots, far_fields):
            residual = []
            for index, (real, imag) in enumerate(far_field):
                power = real * real + imag * imag
                remain = 1.0 - amplitude[slot, index] * lax.rsqrt(
                    jnp.maximum(power, FLOOR * FLOOR)
                )
                residual.append((real * remain, -imag * remain))
            residuals.append(residual)
        backs = [backward(residual, *tables) for residual in residuals]
        probe_terms = [0.0, 0.0]
        for where, (window_real, window_imag), (back_real, back_imag) in zip(places, windows, backs):
            back_imag = -back_imag
            probe_terms[0] += window_real * back_real + window_imag * back_imag
            probe_terms[1] += window_real * back_imag - window_imag * back_real
            add_term(0, probe_real * back_real + probe_imag * back_imag, *where)
            add_term(1, probe_real * back_imag - probe_imag * back_real, *where)
        for part, term in enumerate(probe_terms):
            for piece in range(pieces):
                probe_sum[part, piece] += term[:, LANES * piece : LANES * (piece + 1)]

    def two_patches(index, carry):
        some_patches([2 * index, 2 * index + 1])
        return carry

    count = counts[0]
    lax.fori_loop(0, count // 2, two_patches, 0)

    @pl.when(count % 2 == 1)
    def _():
        some_patches([count - 1])

    given_out[:, :margin] = gradient[:, head, near]
    given_out[:, margin : 2 * margin] = gradient[:, tail, near]
    for part in range(2):
        given_out[part, 2 * margin :] = probe_sum[part, 1 - core[0]]
        probe_out[part] = probe_sum[part, core[0]]
    inner_out[...] = gradient[:, middle, inner]
    up_out[...] = gradient[:, head, inner]
    down_out[...] = gradient[:, tail, inner]
    near_mid_out[...] = gradient[:, middle, near]
    far_mid_out[...] = gradient[:, middle, far]
    far_top_out[...] = gradient[:, head, far]
    far_bottom_out[...] = gradient[:, tail, far]


def patches(counts, rows, cols, core, pieces, probe, amplitude):
    size = probe.shape[1]
    margin = size // 2
    height, width = pieces[0].shape[1:]
    tall, wide = height + size, width + size
    smem = pl.BlockSpec(memory_space=pltpu.SMEM)
    vmem = pl.BlockSpec(memory_space=pltpu.VMEM)
    anywhere = pl.BlockSpec(memory_space=pl.ANY)
    shapes = [
        (height, width),
        (margin, width),
        (margin, width),
        (height, margin),
        (height, margin),
        (2 * margin + size, margin),
        (margin, margin),
        (margin, margin),
        (size, LANES),
    ]
    return pl.pallas_call(
        patch_kernel,
        out_shape=tuple(pltpu.VMEM((2,) + shape, jnp.float32) for shape in shapes),
        in_specs=[smem] * 4 + [anywhere] * 8 + [vmem] * 6,
        out_specs=[vmem] * 9,
        scratch_shapes=[
            pltpu.VMEM((2, tall, wide), jnp.float32),
            pltpu.VMEM((2, tall, wide), jnp.float32),
            pltpu.VMEM((2, size // LANES, size, LANES), jnp.float32),
            pltpu.SemaphoreType.DMA((9,)),
        ],
        compiler_params=pltpu.CompilerParams(vmem_limit_bytes=VMEM_LIMIT),
        name="patches",
    )(
        counts,
        rows,
        cols,
        core,
        *pieces,
        probe,
        amplitude,
        *(jnp.asarray(table) for table in dft_tables(size)),
    )


def haar_kernel(
    core,
    centre,
    inner,
    above,
    below,
    near_top,
    near_bottom,
    far_mid,
    far_top,
    far_bottom,
    out,
    *scratch,
):
    height, width = centre.shape[1:]
    margin = above.shape[1]
    levels = [scratch[level] for level in range(LEVELS)]
    details = [scratch[LEVELS + level] for level in range(LEVELS - 1)]
    columns = width // LANES
    work = levels[0]
    near = (1 - core[0]) * (columns - 1)
    far = core[0] * (columns - 1)
    for part in range(2):
        for column in range(columns):
            piece = part, slice(None), pl.ds(column * LANES, LANES)
            gathered = jnp.concatenate([above[piece], below[piece]], axis=0) + inner[piece]
            work[part, column] = centre[piece] - STEP_OBJECT * gathered
        sides = jnp.concatenate([near_top[part], near_bottom[part]], axis=0)
        work[part, near] -= STEP_OBJECT * sides
        corners = jnp.concatenate([far_top[part], far_bottom[part]], axis=0)
        work[part, far] -= STEP_OBJECT * (far_mid[part] + corners)

    lane = lax.broadcasted_iota(jnp.int32, (TILE, LANES), 1)

    def each(function, *parts):
        return [[function(*pair) for pair in zip(*rows)] for rows in zip(*parts)]

    def level_steps(level):
        stride = 1 << level
        active = lane % stride == 0
        second = lane % (2 * stride) == stride
        keep = jnp.where(active, jnp.where(second, -0.5, 0.5), 1.0).astype(jnp.float32)
        swap = jnp.where(active, 0.5, 0.0).astype(jnp.float32)

        def lane_step(values):
            after = each(lambda value: pltpu.roll(value, LANES - stride, 1), values)
            before = each(lambda value: pltpu.roll(value, stride, 1), values)
            return each(
                lambda value, high, low: value * keep + jnp.where(second, low, high) * swap,
                values,
                after,
                before,
            )

        def row_step(first, other):
            if level == 0:
                return each(jnp.add, first, other), each(jnp.subtract, first, other)
            return (
                each(lambda a, b: jnp.where(active, a + b, a), first, other),
                each(lambda a, b: jnp.where(active, a - b, b), first, other),
            )

        return lane_step, row_step

    def shrink(values, kept=None):
        factors = []
        for real, imag in zip(*values):
            power = real * real + imag * imag
            factor = jnp.maximum(
                1.0 - THRESHOLD * lax.rsqrt(jnp.maximum(power, THRESHOLD * THRESHOLD)), 0.0
            )
            factors.append(factor if kept is None else jnp.where(kept, 1.0, factor))
        return [[value * factor for value, factor in zip(row, factors)] for row in values]

    def load(ref, start, stride=None):
        where = pl.ds(start, TILE) if stride is None else pl.ds(start, TILE, stride=stride)
        return [[ref[part, column, where, :] for column in range(columns)] for part in range(2)]

    def save(ref, values, start, stride=None):
        where = pl.ds(start, TILE) if stride is None else pl.ds(start, TILE, stride=stride)
        for part in range(2):
            for column in range(columns):
                ref[part, column, where, :] = values[part][column]

    for level in range(LEVELS - 1):
        lane_step, row_step = level_steps(level)

        for index in range(height >> (level + 4)):
            base = index * 2 * TILE
            first = load(levels[level], base, 2)
            other = load(levels[level], base + 1, 2)
            low, high = row_step(first, other)
            save(levels[level + 1], lane_step(low), index * TILE)
            save(details[level], shrink(lane_step(high)), index * TILE)

    lane_step, row_step = level_steps(LEVELS - 1)
    coarsest = lane % (1 << LEVELS) == 0
    for index in range(height >> (LEVELS + 3)):
        base = index * 2 * TILE
        low, high = row_step(load(levels[-1], base, 2), load(levels[-1], base + 1, 2))
        low = lane_step(shrink(lane_step(low), coarsest))
        high = lane_step(shrink(lane_step(high)))
        first, other = row_step(low, high)
        save(levels[-1], first, base, 2)
        save(levels[-1], other, base + 1, 2)

    for level in range(LEVELS - 1)[::-1]:
        lane_step, row_step = level_steps(level)
        for index in range(height >> (level + 4)):
            low = lane_step(load(levels[level + 1], index * TILE))
            high = lane_step(load(details[level], index * TILE))
            first, other = row_step(low, high)
            base = index * 2 * TILE
            save(levels[level], first, base, 2)
            save(levels[level], other, base + 1, 2)
    for part in range(2):
        for column in range(columns):
            out[part, :, pl.ds(column * LANES, LANES)] = work[part, column]


def shrink_object(core, *pieces):
    smem = pl.BlockSpec(memory_space=pltpu.SMEM)
    vmem = pl.BlockSpec(memory_space=pltpu.VMEM)
    shape = pieces[0].shape
    sizes = [(2, shape[2] // LANES, shape[1] >> level, LANES) for level in range(LEVELS)]
    return pl.pallas_call(
        haar_kernel,
        out_shape=jax.ShapeDtypeStruct(shape, jnp.float32),
        in_specs=[smem] + [vmem] * len(pieces),
        out_specs=vmem,
        scratch_shapes=[pltpu.VMEM(size, jnp.float32) for size in sizes + sizes[1:]],
        compiler_params=pltpu.CompilerParams(vmem_limit_bytes=VMEM_LIMIT),
        name="haar",
    )(core, *pieces)


def permuted(value, move):
    rows, cols = lax.axis_size("row"), lax.axis_size(AXES[1:])
    pairs = []
    for source in range(rows * cols):
        row, col = move(source // cols, source % cols)
        if 0 <= row < rows and 0 <= col < cols:
            pairs.append((source, row * cols + col))
    return lax.ppermute(value, AXES, pairs)


def up_by(step):
    return lambda row, col: (row + step, col)


def near_to(row, col):
    return row, col ^ 1


def far_to(step):
    return lambda row, col: (row + step, col - 1 if col % 2 == 0 else col + 1)


def chip_tiles(half):
    return half.reshape(lax.axis_size(CHIPS), -1, LANES)


def handed_out(tile):
    tiles = jnp.broadcast_to(tile[None], (lax.axis_size(CHIPS),) + tile.shape)
    return lax.all_to_all(tiles, CHIPS, 0, 0, tiled=True)


def on_device(object_now, object_prev, probe, amplitudes, pos_row, pos_col, counts):
    centre = object_now + MOMENTUM * (object_now - object_prev)
    margin = probe.shape[1] // 2
    height, width = centre.shape[1:]
    slots = amplitudes.shape[2]
    core = lax.axis_index("core")
    core_word = core.reshape(1)
    devices = lax.axis_size(AXES)

    def sides(value):
        first, last = value[:, :, :margin], value[:, :, width - margin :]
        return jnp.where(core == 0, last, first), jnp.where(core == 0, first, last)

    near, far = sides(centre)
    top = permuted(centre[:, height - margin :], up_by(1))
    bottom = permuted(centre[:, :margin], up_by(-1))
    far_top = permuted(far[:, height - margin :], far_to(1))
    far_bottom = permuted(far[:, :margin], far_to(-1))
    far_mid = permuted(far, far_to(0))
    near_mid = permuted(near, near_to)
    near_corner, far_top, far_bottom, far_mid = lax.optimization_barrier(
        (
            jnp.concatenate([sides(top)[0], sides(bottom)[0]], axis=1),
            far_top,
            far_bottom,
            far_mid,
        )
    )
    near_corner = permuted(near_corner, near_to)
    (
        inner,
        up,
        down,
        near_mid,
        far_mid,
        given,
        far_top,
        far_bottom,
        probe_kept,
    ) = patches(
        counts.reshape(1),
        pos_row.reshape(slots),
        pos_col.reshape(slots),
        core_word,
        (centre, top, bottom, near_mid, far_mid, near_corner, far_top, far_bottom),
        probe,
        ordered_amplitude(amplitudes[0, 0]),
    )
    given = permuted(given, near_to)
    corner = given[:, : 2 * margin]
    shares = chip_tiles(probe_kept + given[:, 2 * margin :])

    def with_corner(strip, piece):
        none = jnp.zeros_like(piece)
        first = jnp.where(core == 0, none, piece)
        last = jnp.where(core == 0, piece, none)
        gap = jnp.zeros(piece.shape[:2] + (width - 2 * margin,), piece.dtype)
        return strip + jnp.concatenate([first, gap, last], axis=2)

    up = with_corner(up, corner[:, :margin])
    down = with_corner(down, corner[:, margin:])
    up, down, far_top, far_bottom, far_mid, near_mid, shares = lax.optimization_barrier(
        (up, down, far_top, far_bottom, far_mid, near_mid, shares)
    )
    shares = lax.all_to_all(shares, CHIPS, 0, 0, tiled=True)
    below = permuted(up, up_by(-1))
    above = permuted(down, up_by(1))
    far_below = permuted(far_top, far_to(-1))
    far_above = permuted(far_bottom, far_to(1))
    far_mid = permuted(far_mid, far_to(0))
    near_mid, above, below, far_below, far_above, far_mid = lax.optimization_barrier(
        (near_mid, above, below, far_below, far_above, far_mid)
    )
    near_top = permuted(near_mid[:, :margin], near_to)
    near_top, near_bottom = lax.optimization_barrier((near_top, near_mid[:, margin:]))
    near_bottom = permuted(near_bottom, near_to)
    columns = [probe[:, :, LANES * index : LANES * (index + 1)] for index in range(2)]
    tile = lax.dynamic_index_in_dim(
        chip_tiles(jnp.where(core == 0, *columns)), lax.axis_index(CHIPS), keepdims=False
    )
    tile = tile - PROBE_STEP / (slots * devices) * jnp.sum(shares, axis=0)
    mine = handed_out(tile).reshape(columns[0].shape)
    other = permuted(mine, near_to)
    probe_new = jnp.concatenate(
        [jnp.where(core == 0, mine, other), jnp.where(core == 0, other, mine)], axis=2
    )
    object_new = shrink_object(core_word, centre, inner, above, below, near_top, near_bottom, far_mid, far_above, far_below)
    return object_new, probe_new


def solution(mesh):
    fine = jax.sharding.Mesh(mesh.devices.reshape(mesh.devices.shape[0], -1, 2), AXES)
    col = AXES[1:]
    in_specs = (
        P(None, "row", col),
        P(None, "row", col),
        P(),
        P("row", col, None, None, None),
        P("row", col, None),
        P("row", col, None),
        P("row", col),
    )
    out_specs = (P(None, "row", col), P())
    return jax.shard_map(
        on_device, mesh=fine, in_specs=in_specs, out_specs=out_specs, check_vma=False
    )
```

```python
import math

import jax
import jax.numpy as jnp
import ml_dtypes
import numpy as np
from jax import lax
from jax.experimental import pallas as pl
from jax.experimental.pallas import tpu as pltpu
from jax.sharding import PartitionSpec as P

LEVELS = 4
MOMENTUM = 0.6
STEP_OBJECT = 0.5
PROBE_STEP = 2.0
THRESHOLD = 0.3
FLOOR = 0.5

AXES = ("row", "pair", "core")
CHIPS = ("row", "pair")
LANES = 128
PATCHES = 4
TILE = 8
VMEM_LIMIT = 28 * 1024 * 1024


def split_table(table):
    high = table.astype(ml_dtypes.bfloat16)
    low = (table - high.astype(np.float64)).astype(ml_dtypes.bfloat16)
    return high, low


def dft_tables(length):
    half = length // 2
    points = np.arange(half)
    angles = (points[:, None] * points[None, :] % half) * (-2.0 * math.pi / half)
    real = np.cos(angles) / math.sqrt(length)
    imag = np.sin(angles) / math.sqrt(length)
    left_high, left_low = split_table(np.block([[real, -imag], [imag, real]]))
    right_high, right_low = split_table(np.block([[real, imag], [-imag, real]]))
    turn = points * (-2.0 * math.pi / length)
    twiddle = np.stack([np.cos(turn), np.sin(turn)]).astype(np.float32)
    return (
        np.concatenate([left_high, left_high, left_low], axis=1),
        np.concatenate([right_high, right_high, right_low], axis=0),
        np.repeat(twiddle[:, :, None], LANES, axis=2),
        np.repeat(twiddle[:, None, :], half, axis=1),
    )


def split_value(value):
    high = value.astype(jnp.bfloat16)
    low = (value - high.astype(jnp.float32)).astype(jnp.bfloat16)
    return high, low


def times(real, imag, twiddle):
    cosine, sine = twiddle
    return real * cosine - imag * sine, real * sine + imag * cosine


def left_product(blocks, table):
    half = blocks[0][0].shape[0]
    width = blocks[0][0].shape[1]
    value = jnp.concatenate(
        [jnp.concatenate([real, imag], axis=0) for real, imag in blocks], axis=1
    )
    high, low = split_value(value)
    out = jnp.dot(
        table[...],
        jnp.concatenate([high, low, high], axis=0),
        preferred_element_type=jnp.float32,
    )
    return [
        (out[:half, index * width : (index + 1) * width], out[half:, index * width : (index + 1) * width])
        for index in range(len(blocks))
    ]


def right_product(blocks, table):
    half = blocks[0][0].shape[1]
    value = jnp.concatenate(
        [jnp.concatenate([real, imag], axis=1) for real, imag in blocks], axis=0
    )
    high, low = split_value(value)
    out = jnp.dot(
        jnp.concatenate([high, low, high], axis=1),
        table[...],
        preferred_element_type=jnp.float32,
    )
    return [
        (out[index * half : (index + 1) * half, :half], out[index * half : (index + 1) * half, half:])
        for index in range(len(blocks))
    ]


def forward(real, imag, left_table, right_table, row_twiddle, lane_twiddle):
    half = real.shape[0] // 2
    wide_twiddle = [jnp.concatenate([part, part], axis=1) for part in row_twiddle]
    total = (real[:half] + real[half:], imag[:half] + imag[half:])
    gap = times(real[:half] - real[half:], imag[:half] - imag[half:], wide_twiddle)
    blocks = []
    for real, imag in left_product([total, gap], left_table):
        blocks.append((real[:, :half] + real[:, half:], imag[:, :half] + imag[:, half:]))
        blocks.append(
            times(real[:, :half] - real[:, half:], imag[:, :half] - imag[:, half:], lane_twiddle)
        )
    return right_product(blocks, right_table)


def backward(blocks, left_table, right_table, row_twiddle, lane_twiddle):
    blocks = right_product(blocks, right_table)
    wide_twiddle = [jnp.concatenate([part, part], axis=1) for part in row_twiddle]
    joined = []
    for parity in range(2):
        even_real, even_imag = blocks[2 * parity]
        odd_real, odd_imag = times(*blocks[2 * parity + 1], lane_twiddle)
        joined.append(
            (
                jnp.concatenate([even_real + odd_real, even_real - odd_real], axis=1),
                jnp.concatenate([even_imag + odd_imag, even_imag - odd_imag], axis=1),
            )
        )
    (even_real, even_imag), odd = left_product(joined, left_table)
    odd_real, odd_imag = times(*odd, wide_twiddle)
    return (
        jnp.concatenate([even_real + odd_real, even_real - odd_real], axis=0),
        jnp.concatenate([even_imag + odd_imag, even_imag - odd_imag], axis=0),
    )


def amplitude_kernel(amplitude, table, out, sorted_lanes):
    slots, size, _ = amplitude.shape
    half = size // 2
    for slot in range(slots):
        value = amplitude[slot]
        high = value.astype(jnp.bfloat16)
        rest = value - high.astype(jnp.float32)
        middle, low = split_value(rest)
        ordered = jnp.dot(
            jnp.concatenate([high, middle, low], axis=1),
            table[...],
            preferred_element_type=jnp.float32,
        )
        for index in range(2):
            sorted_lanes[slot, index] = ordered[:, index * half : (index + 1) * half]
            for parity in range(2):
                out[slot, 2 * parity + index] = sorted_lanes[slot, index, pl.ds(parity, half, stride=2), :]


def ordered_amplitude(amplitude):
    slots, size, _ = amplitude.shape
    half = size // 2
    table = np.zeros((size, size), np.float32)
    table[2 * np.arange(half), np.arange(half)] = 1
    table[2 * np.arange(half) + 1, half + np.arange(half)] = 1
    table = np.concatenate([table] * 3, axis=0).astype(ml_dtypes.bfloat16)
    vmem = pl.BlockSpec(memory_space=pltpu.VMEM)
    return pl.pallas_call(
        amplitude_kernel,
        out_shape=pltpu.VMEM((slots, 4, half, half), jnp.float32),
        in_specs=[vmem, vmem],
        out_specs=vmem,
        scratch_shapes=[pltpu.VMEM((slots, 2, size, half), jnp.float32)],
        compiler_params=pltpu.CompilerParams(vmem_limit_bytes=VMEM_LIMIT),
        cost_estimate=pl.CostEstimate(
            flops=2 * slots * size**3 * 3, bytes_accessed=8 * slots * size**2, transcendentals=0
        ),
        name="ordered_amplitude",
    )(amplitude, jnp.asarray(table))


def patch_kernel(
    counts,
    rows,
    cols,
    place_of,
    centre,
    top,
    bottom,
    near_mid,
    far_mid,
    near_corner,
    far_top,
    far_bottom,
    probe,
    amplitude,
    left_table,
    right_table,
    row_table,
    lane_table,
    inner_out,
    first_out,
    second_out,
    near_mid_out,
    far_mid_out,
    given_out,
    far_top_out,
    far_bottom_out,
    probe_out,
    extended,
    gradient,
    probe_sum,
    sems,
):
    size = probe.shape[1]
    margin = size // 2
    height, width = centre.shape[1:]
    inner = pl.ds(margin, width)
    core, odd = place_of[0], place_of[1]
    near = pl.ds(pl.multiple_of((1 - core) * (margin + width), LANES), margin)
    far = pl.ds(pl.multiple_of(core * (margin + width), LANES), margin)
    first = pl.ds(pl.multiple_of((1 - odd) * (margin + height), margin), margin)
    second = pl.ds(pl.multiple_of(odd * (margin + height), margin), margin)
    head, middle, tail = pl.ds(0, margin), pl.ds(margin, height), pl.ds(margin + height, margin)
    moves = [
        (centre, extended.at[:, middle, inner]),
        (near_mid, extended.at[:, middle, near]),
        (far_mid, extended.at[:, middle, far]),
        (top, extended.at[:, head, inner]),
        (bottom, extended.at[:, tail, inner]),
        (far_top, extended.at[:, head, far]),
        (far_bottom, extended.at[:, tail, far]),
        (near_corner.at[:, head, :], extended.at[:, head, near]),
        (near_corner.at[:, pl.ds(margin, margin), :], extended.at[:, tail, near]),
    ]
    copies = [
        pltpu.make_async_copy(source, target, sems.at[index])
        for index, (source, target) in enumerate(moves)
    ]
    for copy in copies:
        copy.start()
    gradient[...] = jnp.zeros_like(gradient)
    probe_sum[...] = jnp.zeros_like(probe_sum)
    for copy in copies:
        copy.wait()
    tile = (1, TILE, LANES)
    lane = lax.broadcasted_iota(jnp.int32, tile, 2)
    sublane = lax.broadcasted_iota(jnp.int32, tile, 1)
    tiles = size // TILE
    pieces = size // LANES

    tables = (
        left_table,
        right_table,
        (row_table[0], row_table[1]),
        (lane_table[0], lane_table[1]),
    )

    def place(slot):
        row_shift = lax.rem(rows[slot], TILE)
        col_shift = lax.rem(cols[slot], LANES)
        row = pl.multiple_of(rows[slot] - row_shift, TILE)
        col = pl.multiple_of(cols[slot] - col_shift, LANES)
        areas = [
            (pl.ds(row, size + TILE), pl.ds(col + LANES * piece, LANES))
            for piece in range(pieces + 1)
        ]
        return row_shift, col_shift, areas

    def window(part, row_shift, col_shift, areas):
        columns = [
            pltpu.roll(
                extended[(part,) + area].reshape(tiles + 1, TILE, LANES),
                lax.rem(LANES - col_shift, LANES),
                2,
            )
            for area in areas
        ]
        result = []
        for piece in range(pieces):
            value = jnp.where(lane < LANES - col_shift, columns[piece], columns[piece + 1])
            value = pltpu.roll(value, lax.rem(TILE - row_shift, TILE), 1)
            value = jnp.where(sublane < TILE - row_shift, value[:tiles], value[1:])
            result.append(value.reshape(size, LANES))
        return jnp.concatenate(result, axis=1)

    def add_term(part, term, row_shift, col_shift, areas):
        columns = []
        ended = jnp.zeros(tile, jnp.float32)
        for piece in range(pieces):
            value = term[:, LANES * piece : LANES * (piece + 1)].reshape(tiles, TILE, LANES)
            value = pltpu.roll(value, row_shift, 1)
            value = jnp.where(
                sublane >= row_shift,
                jnp.concatenate([value, ended], axis=0),
                jnp.concatenate([ended, value], axis=0),
            )
            columns.append(pltpu.roll(value, col_shift, 2))
        ended = jnp.zeros_like(columns[0])
        columns = [ended] + columns + [ended]
        for piece, area in enumerate(areas):
            block = jnp.where(lane >= col_shift, columns[piece + 1], columns[piece])
            gradient[(part,) + area] += block.reshape(size + TILE, LANES)

    def some_patches(slots):
        places = [place(slot) for slot in slots]
        windows = [[window(part, *where) for part in range(2)] for where in places]
        probe_real = probe[0]
        probe_imag = probe[1]
        far_fields = [
            forward(
                probe_real * real - probe_imag * imag, probe_real * imag + probe_imag * real, *tables
            )
            for real, imag in windows
        ]
        residuals = []
        for slot, far_field in zip(slots, far_fields):
            residual = []
            for index, (real, imag) in enumerate(far_field):
                power = real * real + imag * imag
                remain = 1.0 - amplitude[slot, index] * lax.rsqrt(
                    jnp.maximum(power, FLOOR * FLOOR)
                )
                residual.append((real * remain, -imag * remain))
            residuals.append(residual)
        backs = [backward(residual, *tables) for residual in residuals]
        probe_terms = [0.0, 0.0]
        for where, (window_real, window_imag), (back_real, back_imag) in zip(places, windows, backs):
            back_imag = -back_imag
            probe_terms[0] += window_real * back_real + window_imag * back_imag
            probe_terms[1] += window_real * back_imag - window_imag * back_real
            add_term(0, probe_real * back_real + probe_imag * back_imag, *where)
            add_term(1, probe_real * back_imag - probe_imag * back_real, *where)
        for part, term in enumerate(probe_terms):
            for piece in range(pieces):
                probe_sum[part, piece] += term[:, LANES * piece : LANES * (piece + 1)]

    def two_patches(index, carry):
        some_patches([2 * index, 2 * index + 1])
        return carry

    count = counts[0]
    lax.fori_loop(0, count // 2, two_patches, 0)

    @pl.when(count % 2 == 1)
    def _():
        some_patches([count - 1])

    given_out[:, :margin] = gradient[:, first, near]
    given_out[:, margin : 2 * margin] = gradient[:, second, near]
    for part in range(2):
        given_out[part, 2 * margin :] = probe_sum[part, 1 - core]
        probe_out[part] = probe_sum[part, core]
    inner_out[...] = gradient[:, middle, inner]
    first_out[...] = gradient[:, first, inner]
    second_out[...] = gradient[:, second, inner]
    near_mid_out[...] = gradient[:, middle, near]
    far_mid_out[...] = gradient[:, middle, far]
    far_top_out[...] = gradient[:, head, far]
    far_bottom_out[...] = gradient[:, tail, far]


def patches(counts, rows, cols, place_of, pieces, probe, amplitude):
    size = probe.shape[1]
    margin = size // 2
    height, width = pieces[0].shape[1:]
    tall, wide = height + size, width + size
    smem = pl.BlockSpec(memory_space=pltpu.SMEM)
    vmem = pl.BlockSpec(memory_space=pltpu.VMEM)
    anywhere = pl.BlockSpec(memory_space=pl.ANY)
    shapes = [
        (height, width),
        (margin, width),
        (margin, width),
        (height, margin),
        (height, margin),
        (2 * margin + size, margin),
        (margin, margin),
        (margin, margin),
        (size, LANES),
    ]
    return pl.pallas_call(
        patch_kernel,
        out_shape=tuple(pltpu.VMEM((2,) + shape, jnp.float32) for shape in shapes),
        in_specs=[smem] * 4 + [anywhere] * 8 + [vmem] * 6,
        out_specs=[vmem] * 9,
        scratch_shapes=[
            pltpu.VMEM((2, tall, wide), jnp.float32),
            pltpu.VMEM((2, tall, wide), jnp.float32),
            pltpu.VMEM((2, size // LANES, size, LANES), jnp.float32),
            pltpu.SemaphoreType.DMA((9,)),
        ],
        compiler_params=pltpu.CompilerParams(vmem_limit_bytes=VMEM_LIMIT),
        name="patches",
    )(
        counts,
        rows,
        cols,
        place_of,
        *pieces,
        probe,
        amplitude,
        *(jnp.asarray(table) for table in dft_tables(size)),
    )


def haar_kernel(
    place_of,
    centre,
    inner,
    first,
    second,
    near_mid,
    far_mid,
    far_top,
    far_bottom,
    out,
    *scratch,
):
    height, width = centre.shape[1:]
    margin = first.shape[1]
    core, odd = place_of[0], place_of[1]
    levels = [scratch[level] for level in range(LEVELS)]
    details = [scratch[LEVELS + level] for level in range(LEVELS - 1)]
    columns = width // LANES
    work = levels[0]
    near = (1 - core) * (columns - 1)
    far = core * (columns - 1)
    first_rows = pl.ds(pl.multiple_of((1 - odd) * (height - margin), margin), margin)
    second_rows = pl.ds(pl.multiple_of(odd * (height - margin), margin), margin)
    for part in range(2):
        for column in range(columns):
            piece = part, slice(None), pl.ds(column * LANES, LANES)
            work[part, column] = centre[piece] - STEP_OBJECT * inner[piece]
            work[part, column, first_rows] -= STEP_OBJECT * first[piece]
            work[part, column, second_rows] -= STEP_OBJECT * second[piece]
        work[part, near] -= STEP_OBJECT * near_mid[part]
        corners = jnp.concatenate([far_top[part], far_bottom[part]], axis=0)
        work[part, far] -= STEP_OBJECT * (far_mid[part] + corners)

    lane = lax.broadcasted_iota(jnp.int32, (TILE, LANES), 1)

    def each(function, *parts):
        return [[function(*pair) for pair in zip(*rows)] for rows in zip(*parts)]

    def level_steps(level):
        stride = 1 << level
        active = lane % stride == 0
        second = lane % (2 * stride) == stride
        keep = jnp.where(active, jnp.where(second, -0.5, 0.5), 1.0).astype(jnp.float32)
        swap = jnp.where(active, 0.5, 0.0).astype(jnp.float32)

        def lane_step(values):
            after = each(lambda value: pltpu.roll(value, LANES - stride, 1), values)
            before = each(lambda value: pltpu.roll(value, stride, 1), values)
            return each(
                lambda value, high, low: value * keep + jnp.where(second, low, high) * swap,
                values,
                after,
                before,
            )

        def row_step(first, other):
            if level == 0:
                return each(jnp.add, first, other), each(jnp.subtract, first, other)
            return (
                each(lambda a, b: jnp.where(active, a + b, a), first, other),
                each(lambda a, b: jnp.where(active, a - b, b), first, other),
            )

        return lane_step, row_step

    def shrink(values, kept=None):
        factors = []
        for real, imag in zip(*values):
            power = real * real + imag * imag
            factor = jnp.maximum(
                1.0 - THRESHOLD * lax.rsqrt(jnp.maximum(power, THRESHOLD * THRESHOLD)), 0.0
            )
            factors.append(factor if kept is None else jnp.where(kept, 1.0, factor))
        return [[value * factor for value, factor in zip(row, factors)] for row in values]

    def load(ref, start, stride=None):
        where = pl.ds(start, TILE) if stride is None else pl.ds(start, TILE, stride=stride)
        return [[ref[part, column, where, :] for column in range(columns)] for part in range(2)]

    def save(ref, values, start, stride=None):
        where = pl.ds(start, TILE) if stride is None else pl.ds(start, TILE, stride=stride)
        for part in range(2):
            for column in range(columns):
                ref[part, column, where, :] = values[part][column]

    for level in range(LEVELS - 1):
        lane_step, row_step = level_steps(level)

        for index in range(height >> (level + 4)):
            base = index * 2 * TILE
            first = load(levels[level], base, 2)
            other = load(levels[level], base + 1, 2)
            low, high = row_step(first, other)
            save(levels[level + 1], lane_step(low), index * TILE)
            save(details[level], shrink(lane_step(high)), index * TILE)

    lane_step, row_step = level_steps(LEVELS - 1)
    coarsest = lane % (1 << LEVELS) == 0
    for index in range(height >> (LEVELS + 3)):
        base = index * 2 * TILE
        low, high = row_step(load(levels[-1], base, 2), load(levels[-1], base + 1, 2))
        low = lane_step(shrink(lane_step(low), coarsest))
        high = lane_step(shrink(lane_step(high)))
        first, other = row_step(low, high)
        save(levels[-1], first, base, 2)
        save(levels[-1], other, base + 1, 2)

    for level in range(LEVELS - 1)[::-1]:
        lane_step, row_step = level_steps(level)
        for index in range(height >> (level + 4)):
            low = lane_step(load(levels[level + 1], index * TILE))
            high = lane_step(load(details[level], index * TILE))
            first, other = row_step(low, high)
            base = index * 2 * TILE
            save(levels[level], first, base, 2)
            save(levels[level], other, base + 1, 2)
    for part in range(2):
        for column in range(columns):
            out[part, :, pl.ds(column * LANES, LANES)] = work[part, column]


def shrink_object(place_of, *pieces):
    smem = pl.BlockSpec(memory_space=pltpu.SMEM)
    vmem = pl.BlockSpec(memory_space=pltpu.VMEM)
    shape = pieces[0].shape
    sizes = [(2, shape[2] // LANES, shape[1] >> level, LANES) for level in range(LEVELS)]
    return pl.pallas_call(
        haar_kernel,
        out_shape=jax.ShapeDtypeStruct(shape, jnp.float32),
        in_specs=[smem] + [vmem] * len(pieces),
        out_specs=vmem,
        scratch_shapes=[pltpu.VMEM(size, jnp.float32) for size in sizes + sizes[1:]],
        compiler_params=pltpu.CompilerParams(vmem_limit_bytes=VMEM_LIMIT),
        name="haar",
    )(place_of, *pieces)


def join_kernel(place_of, first, second, given, kept, first_out, second_out, shares):
    margin = first.shape[1]
    width = first.shape[2]
    near = pl.ds(pl.multiple_of((1 - place_of[0]) * (width - LANES), LANES), LANES)
    first_out[...] = first[...]
    second_out[...] = second[...]
    first_out[:, :, near] += given[:, :margin]
    second_out[:, :, near] += given[:, margin : 2 * margin]
    shares[...] = (kept[...] + given[:, 2 * margin :]).reshape(shares.shape)


def joined(place_of, first, second, given, kept):
    smem = pl.BlockSpec(memory_space=pltpu.SMEM)
    vmem = pl.BlockSpec(memory_space=pltpu.VMEM)
    shapes = [first.shape, second.shape, (kept.size // (TILE * LANES), TILE, LANES)]
    return pl.pallas_call(
        join_kernel,
        out_shape=tuple(jax.ShapeDtypeStruct(shape, jnp.float32) for shape in shapes),
        in_specs=[smem] + [vmem] * 4,
        out_specs=[vmem] * 3,
        compiler_params=pltpu.CompilerParams(vmem_limit_bytes=VMEM_LIMIT),
        name="joined",
    )(place_of, first, second, given, kept)


def total_kernel(shares, tile, out):
    total = shares[0]
    for index in range(1, shares.shape[0]):
        total = total + shares[index]
    total = tile[...] - total * (PROBE_STEP / (PATCHES * out.shape[0]))
    for index in range(out.shape[0]):
        out[index] = total


def new_tiles(shares, tile, devices):
    vmem = pl.BlockSpec(memory_space=pltpu.VMEM)
    return pl.pallas_call(
        total_kernel,
        out_shape=jax.ShapeDtypeStruct((devices,) + tile.shape, jnp.float32),
        in_specs=[vmem] * 2,
        out_specs=vmem,
        compiler_params=pltpu.CompilerParams(vmem_limit_bytes=VMEM_LIMIT),
        name="new_tiles",
    )(shares, tile)


def probe_kernel(tiles, out):
    size = out.shape[1]
    chips = size // TILE
    for part in range(2):
        for half in range(2):
            value = tiles[pl.ds(part * chips, chips), half]
            out[part, :, pl.ds(half * LANES, LANES)] = value.reshape(size, LANES)


def laid_out(tiles, shape):
    vmem = pl.BlockSpec(memory_space=pltpu.VMEM)
    return pl.pallas_call(
        probe_kernel,
        out_shape=jax.ShapeDtypeStruct(shape, jnp.float32),
        in_specs=[vmem],
        out_specs=vmem,
        compiler_params=pltpu.CompilerParams(vmem_limit_bytes=VMEM_LIMIT),
        name="laid_out",
    )(tiles)


def permuted(value, move):
    rows, cols = lax.axis_size("row"), lax.axis_size(AXES[1:])
    pairs = []
    for source in range(rows * cols):
        row, col = move(source // cols, source % cols)
        if 0 <= row < rows and 0 <= col < cols:
            pairs.append((source, row * cols + col))
    return lax.ppermute(value, AXES, pairs)


def up_by(step):
    return lambda row, col: (row + step, col)


def near_to(row, col):
    return row, col ^ 1


def far_to(step):
    return lambda row, col: (row + step, col - 1 if col % 2 == 0 else col + 1)


def chip_tiles(half):
    return half.reshape(lax.axis_size(CHIPS), -1, LANES)


def pair_to(first):
    return lambda row, col: (row + (1 if (row % 2 == 0) == first else -1), col)


def on_device(object_now, object_prev, probe, amplitudes, pos_row, pos_col, counts):
    centre = object_now + MOMENTUM * (object_now - object_prev)
    margin = probe.shape[1] // 2
    height, width = centre.shape[1:]
    slots = amplitudes.shape[2]
    core = lax.axis_index("core")
    odd = lax.axis_index("row") % 2
    place_of = jnp.stack([core, odd])

    def sides(value):
        first, last = value[:, :, :margin], value[:, :, width - margin :]
        return jnp.where(core == 0, last, first), jnp.where(core == 0, first, last)

    near, far = sides(centre)
    top = permuted(centre[:, height - margin :], up_by(1))
    bottom = permuted(centre[:, :margin], up_by(-1))
    far_top = permuted(far[:, height - margin :], far_to(1))
    far_bottom = permuted(far[:, :margin], far_to(-1))
    far_mid = permuted(far, far_to(0))
    near_mid = permuted(near, near_to)
    near_corner, far_top, far_bottom, far_mid = lax.optimization_barrier(
        (
            jnp.concatenate([sides(top)[0], sides(bottom)[0]], axis=1),
            far_top,
            far_bottom,
            far_mid,
        )
    )
    near_corner = permuted(near_corner, near_to)
    (
        inner,
        first,
        second,
        near_mid,
        far_mid,
        given,
        far_top,
        far_bottom,
        probe_kept,
    ) = patches(
        counts.reshape(1),
        pos_row.reshape(slots),
        pos_col.reshape(slots),
        place_of,
        (centre, top, bottom, near_mid, far_mid, near_corner, far_top, far_bottom),
        probe,
        ordered_amplitude(amplitudes[0, 0]),
    )
    given = permuted(given, near_to)
    first, second, shares = joined(place_of, first, second, given, probe_kept)
    first, second, far_top, far_bottom, far_mid, near_mid, shares = lax.optimization_barrier(
        (first, second, far_top, far_bottom, far_mid, near_mid, shares)
    )
    first = permuted(first, pair_to(True))
    first, second = lax.optimization_barrier((first, second))
    second = permuted(second, pair_to(False))
    far_below = permuted(far_top, far_to(-1))
    far_above = permuted(far_bottom, far_to(1))
    far_mid = permuted(far_mid, far_to(0))
    near_mid, first, second, far_below, far_above, far_mid = lax.optimization_barrier(
        (near_mid, first, second, far_below, far_above, far_mid)
    )
    near_mid = permuted(near_mid, near_to)
    shares = lax.all_to_all(shares, CHIPS, 0, 0, tiled=True)
    columns = [probe[:, :, LANES * index : LANES * (index + 1)] for index in range(2)]
    tile = lax.dynamic_index_in_dim(
        chip_tiles(jnp.where(core == 0, *columns)), lax.axis_index(CHIPS), keepdims=False
    )
    tiles = new_tiles(shares, tile, lax.axis_size(AXES))
    tiles = lax.all_to_all(tiles, AXES, 0, 0, tiled=True)
    probe_new = laid_out(tiles.reshape(-1, 2, TILE, LANES), probe.shape)
    object_new = shrink_object(
        place_of, centre, inner, first, second, near_mid, far_mid, far_above, far_below
    )
    return object_new, probe_new


def solution(mesh):
    fine = jax.sharding.Mesh(mesh.devices.reshape(mesh.devices.shape[0], -1, 2), AXES)
    col = AXES[1:]
    in_specs = (
        P(None, "row", col),
        P(None, "row", col),
        P(),
        P("row", col, None, None, None),
        P("row", col, None),
        P("row", col, None),
        P("row", col),
    )
    out_specs = (P(None, "row", col), P())
    return jax.shard_map(
        on_device, mesh=fine, in_specs=in_specs, out_specs=out_specs, check_vma=False
    )
```

```python
import math

import jax
import jax.numpy as jnp
import ml_dtypes
import numpy as np
from jax import lax
from jax.experimental import pallas as pl
from jax.experimental.pallas import tpu as pltpu
from jax.sharding import PartitionSpec as P

LEVELS = 4
MOMENTUM = 0.6
STEP_OBJECT = 0.5
PROBE_STEP = 2.0
THRESHOLD = 0.3
FLOOR = 0.5

ROW = ("z", "xh")
COL = ("y", "xl", "core")
AXES = ROW + COL
CHIPS = ROW + COL[:2]
LANES = 128
PATCHES = 4
DEVICES = 128
TILE = 8
MIB = 1024 * 1024


def split_table(table):
    high = table.astype(ml_dtypes.bfloat16)
    low = (table - high.astype(np.float64)).astype(ml_dtypes.bfloat16)
    return high, low


def dft_tables(length):
    half = length // 2
    points = np.arange(half)
    angles = (points[:, None] * points[None, :] % half) * (-2.0 * math.pi / half)
    real = np.cos(angles) / math.sqrt(length)
    imag = np.sin(angles) / math.sqrt(length)
    left_high, left_low = split_table(np.block([[real, -imag], [imag, real]]))
    right_high, right_low = split_table(np.block([[real, imag], [-imag, real]]))
    turn = points * (-2.0 * math.pi / length)
    twiddle = np.stack([np.cos(turn), np.sin(turn)]).astype(np.float32)
    return (
        np.concatenate([left_high, left_high, left_low], axis=1),
        np.concatenate([right_high, right_high, right_low], axis=0),
        np.concatenate(
            [np.repeat(twiddle[:, :, None], LANES, axis=2), np.repeat(twiddle[:, None, :], half, axis=1)]
        ),
    )


def split_value(value):
    high = value.astype(jnp.bfloat16)
    low = (value - high.astype(jnp.float32)).astype(jnp.bfloat16)
    return high, low


def times(real, imag, twiddle):
    cosine, sine = twiddle
    return real * cosine - imag * sine, real * sine + imag * cosine


def left_product(blocks, table):
    half = blocks[0][0].shape[0]
    width = blocks[0][0].shape[1]
    value = jnp.concatenate(
        [jnp.concatenate([real, imag], axis=0) for real, imag in blocks], axis=1
    )
    high, low = split_value(value)
    out = jnp.dot(
        table[...],
        jnp.concatenate([high, low, high], axis=0),
        preferred_element_type=jnp.float32,
    )
    return [
        (out[:half, index * width : (index + 1) * width], out[half:, index * width : (index + 1) * width])
        for index in range(len(blocks))
    ]


def right_product(blocks, table):
    half = blocks[0][0].shape[1]
    value = jnp.concatenate(
        [jnp.concatenate([real, imag], axis=1) for real, imag in blocks], axis=0
    )
    high, low = split_value(value)
    out = jnp.dot(
        jnp.concatenate([high, low, high], axis=1),
        table[...],
        preferred_element_type=jnp.float32,
    )
    return [
        (out[index * half : (index + 1) * half, :half], out[index * half : (index + 1) * half, half:])
        for index in range(len(blocks))
    ]


def forward(real, imag, left_table, right_table, row_twiddle, lane_twiddle):
    half = real.shape[0] // 2
    wide_twiddle = [jnp.concatenate([part, part], axis=1) for part in row_twiddle]
    total = (real[:half] + real[half:], imag[:half] + imag[half:])
    gap = times(real[:half] - real[half:], imag[:half] - imag[half:], wide_twiddle)
    blocks = []
    for real, imag in left_product([total, gap], left_table):
        blocks.append((real[:, :half] + real[:, half:], imag[:, :half] + imag[:, half:]))
        blocks.append(
            times(real[:, :half] - real[:, half:], imag[:, :half] - imag[:, half:], lane_twiddle)
        )
    return right_product(blocks, right_table)


def backward(blocks, left_table, right_table, row_twiddle, lane_twiddle):
    blocks = right_product(blocks, right_table)
    wide_twiddle = [jnp.concatenate([part, part], axis=1) for part in row_twiddle]
    joined = []
    for parity in range(2):
        even_real, even_imag = blocks[2 * parity]
        odd_real, odd_imag = times(*blocks[2 * parity + 1], lane_twiddle)
        joined.append(
            (
                jnp.concatenate([even_real + odd_real, even_real - odd_real], axis=1),
                jnp.concatenate([even_imag + odd_imag, even_imag - odd_imag], axis=1),
            )
        )
    (even_real, even_imag), odd = left_product(joined, left_table)
    odd_real, odd_imag = times(*odd, wide_twiddle)
    return (
        jnp.concatenate([even_real + odd_real, even_real - odd_real], axis=0),
        jnp.concatenate([even_imag + odd_imag, even_imag - odd_imag], axis=0),
    )


def amplitude_kernel(amplitude, table, out, sorted_lanes):
    slots, size, _ = amplitude.shape
    half = size // 2
    for slot in range(slots):
        value = amplitude[slot]
        high = value.astype(jnp.bfloat16)
        rest = value - high.astype(jnp.float32)
        middle, low = split_value(rest)
        ordered = jnp.dot(
            jnp.concatenate([high, middle, low], axis=1),
            table[...],
            preferred_element_type=jnp.float32,
        )
        for index in range(2):
            sorted_lanes[slot, index] = ordered[:, index * half : (index + 1) * half]
            for parity in range(2):
                out[slot, 2 * parity + index] = sorted_lanes[slot, index, pl.ds(parity, half, stride=2), :]


def ordered_amplitude(amplitude):
    slots, size, _ = amplitude.shape
    half = size // 2
    table = np.zeros((size, size), np.float32)
    table[2 * np.arange(half), np.arange(half)] = 1
    table[2 * np.arange(half) + 1, half + np.arange(half)] = 1
    table = np.concatenate([table] * 3, axis=0).astype(ml_dtypes.bfloat16)
    vmem = pl.BlockSpec(memory_space=pltpu.VMEM)
    return pl.pallas_call(
        amplitude_kernel,
        out_shape=jax.ShapeDtypeStruct((slots, 4, half, half), jnp.float32),
        in_specs=[vmem, vmem],
        out_specs=vmem,
        scratch_shapes=[pltpu.VMEM((slots, 2, size, half), jnp.float32)],
        compiler_params=pltpu.CompilerParams(vmem_limit_bytes=8 * MIB),
        cost_estimate=pl.CostEstimate(
            flops=2 * slots * size**3 * 3, bytes_accessed=8 * slots * size**2, transcendentals=0
        ),
        name="ordered_amplitude",
    )(amplitude, jnp.asarray(table))


def patch_kernel(
    counts,
    rows,
    cols,
    core_of,
    odd_of,
    centre,
    top,
    bottom,
    near_mid,
    far_mid,
    near_corner,
    far_top,
    far_bottom,
    probe,
    amplitude,
    left_table,
    right_table,
    twiddle_table,
    inner_out,
    first_out,
    second_out,
    near_mid_out,
    far_mid_out,
    given_out,
    far_top_out,
    far_bottom_out,
    probe_out,
    extended,
    gradient,
    probe_sum,
    sems,
):
    size = probe.shape[1]
    margin = size // 2
    height, width = centre.shape[1:]
    inner = pl.ds(margin, width)
    core, odd = core_of[0], odd_of[0]
    near = pl.ds(pl.multiple_of((1 - core) * (margin + width), LANES), margin)
    far = pl.ds(pl.multiple_of(core * (margin + width), LANES), margin)
    first = pl.ds(pl.multiple_of((1 - odd) * (margin + height), margin), margin)
    second = pl.ds(pl.multiple_of(odd * (margin + height), margin), margin)
    head, middle, tail = pl.ds(0, margin), pl.ds(margin, height), pl.ds(margin + height, margin)
    moves = [
        (centre, extended.at[:, middle, inner]),
        (near_mid, extended.at[:, middle, near]),
        (far_mid, extended.at[:, middle, far]),
        (top, extended.at[:, head, inner]),
        (bottom, extended.at[:, tail, inner]),
        (far_top, extended.at[:, head, far]),
        (far_bottom, extended.at[:, tail, far]),
        (near_corner.at[:, head, :], extended.at[:, head, near]),
        (near_corner.at[:, pl.ds(margin, margin), :], extended.at[:, tail, near]),
    ]
    copies = [
        pltpu.make_async_copy(source, target, sems.at[index])
        for index, (source, target) in enumerate(moves)
    ]
    for copy in copies:
        copy.start()
    gradient[...] = jnp.zeros_like(gradient)
    probe_sum[...] = jnp.zeros_like(probe_sum)
    for copy in copies:
        copy.wait()
    tile = (1, TILE, LANES)
    lane = lax.broadcasted_iota(jnp.int32, tile, 2)
    sublane = lax.broadcasted_iota(jnp.int32, tile, 1)
    tiles = size // TILE
    pieces = size // LANES

    tables = (
        left_table,
        right_table,
        (twiddle_table[0], twiddle_table[1]),
        (twiddle_table[2], twiddle_table[3]),
    )

    def place(slot):
        row_shift = lax.rem(rows[slot], TILE)
        col_shift = lax.rem(cols[slot], LANES)
        row = pl.multiple_of(rows[slot] - row_shift, TILE)
        col = pl.multiple_of(cols[slot] - col_shift, LANES)
        areas = [
            (pl.ds(row, size + TILE), pl.ds(col + LANES * piece, LANES))
            for piece in range(pieces + 1)
        ]
        return row_shift, col_shift, areas

    def window(part, row_shift, col_shift, areas):
        columns = [
            pltpu.roll(
                extended[(part,) + area].reshape(tiles + 1, TILE, LANES),
                lax.rem(LANES - col_shift, LANES),
                2,
            )
            for area in areas
        ]
        result = []
        for piece in range(pieces):
            value = jnp.where(lane < LANES - col_shift, columns[piece], columns[piece + 1])
            value = pltpu.roll(value, lax.rem(TILE - row_shift, TILE), 1)
            value = jnp.where(sublane < TILE - row_shift, value[:tiles], value[1:])
            result.append(value.reshape(size, LANES))
        return jnp.concatenate(result, axis=1)

    def add_term(part, term, row_shift, col_shift, areas):
        columns = []
        ended = jnp.zeros(tile, jnp.float32)
        for piece in range(pieces):
            value = term[:, LANES * piece : LANES * (piece + 1)].reshape(tiles, TILE, LANES)
            value = pltpu.roll(value, row_shift, 1)
            value = jnp.where(
                sublane >= row_shift,
                jnp.concatenate([value, ended], axis=0),
                jnp.concatenate([ended, value], axis=0),
            )
            columns.append(pltpu.roll(value, col_shift, 2))
        ended = jnp.zeros_like(columns[0])
        columns = [ended] + columns + [ended]
        for piece, area in enumerate(areas):
            block = jnp.where(lane >= col_shift, columns[piece + 1], columns[piece])
            gradient[(part,) + area] += block.reshape(size + TILE, LANES)

    def some_patches(slots):
        places = [place(slot) for slot in slots]
        windows = [[window(part, *where) for part in range(2)] for where in places]
        probe_real = probe[0]
        probe_imag = probe[1]
        far_fields = [
            forward(
                probe_real * real - probe_imag * imag, probe_real * imag + probe_imag * real, *tables
            )
            for real, imag in windows
        ]
        residuals = []
        for slot, far_field in zip(slots, far_fields):
            residual = []
            for index, (real, imag) in enumerate(far_field):
                power = real * real + imag * imag
                remain = 1.0 - amplitude[slot, index] * lax.rsqrt(
                    jnp.maximum(power, FLOOR * FLOOR)
                )
                residual.append((real * remain, -imag * remain))
            residuals.append(residual)
        backs = [backward(residual, *tables) for residual in residuals]
        probe_terms = [0.0, 0.0]
        for where, (window_real, window_imag), (back_real, back_imag) in zip(places, windows, backs):
            back_imag = -back_imag
            probe_terms[0] += window_real * back_real + window_imag * back_imag
            probe_terms[1] += window_real * back_imag - window_imag * back_real
            add_term(0, probe_real * back_real + probe_imag * back_imag, *where)
            add_term(1, probe_real * back_imag - probe_imag * back_real, *where)
        for part, term in enumerate(probe_terms):
            for piece in range(pieces):
                probe_sum[part, piece] += term[:, LANES * piece : LANES * (piece + 1)]

    def two_patches(index, carry):
        some_patches([2 * index, 2 * index + 1])
        return carry

    count = counts[0]
    lax.fori_loop(0, count // 2, two_patches, 0)

    @pl.when(count % 2 == 1)
    def _():
        some_patches([count - 1])

    gradient[:, middle, inner] = (
        extended[:, middle, inner] - STEP_OBJECT * gradient[:, middle, inner]
    )
    inner_copy = pltpu.make_async_copy(gradient.at[:, middle, inner], inner_out, sems.at[0])
    inner_copy.start()
    given_out[:, :margin] = gradient[:, first, near]
    given_out[:, margin : 2 * margin] = gradient[:, second, near]
    for part in range(2):
        given_out[part, 2 * margin :] = probe_sum[part, 1 - core]
        probe_out[part] = probe_sum[part, core]
    first_out[...] = gradient[:, first, inner]
    second_out[...] = gradient[:, second, inner]
    near_mid_out[...] = gradient[:, middle, near]
    far_mid_out[...] = gradient[:, middle, far]
    far_top_out[...] = gradient[:, head, far]
    far_bottom_out[...] = gradient[:, tail, far]
    inner_copy.wait()


def patches(counts, rows, cols, place_of, pieces, probe, amplitude):
    size = probe.shape[1]
    margin = size // 2
    height, width = pieces[0].shape[1:]
    tall, wide = height + size, width + size
    smem = pl.BlockSpec(memory_space=pltpu.SMEM)
    vmem = pl.BlockSpec(memory_space=pltpu.VMEM)
    anywhere = pl.BlockSpec(memory_space=pl.ANY)
    shapes = [
        (height, width),
        (margin, width),
        (margin, width),
        (height, margin),
        (height, margin),
        (2 * margin + size, margin),
        (margin, margin),
        (margin, margin),
        (size, LANES),
    ]
    return pl.pallas_call(
        patch_kernel,
        out_shape=tuple(jax.ShapeDtypeStruct((2,) + shape, jnp.float32) for shape in shapes),
        in_specs=[smem] * 5 + [anywhere] * 8 + [vmem] * 5,
        out_specs=[anywhere] + [vmem] * 8,
        scratch_shapes=[
            pltpu.VMEM((2, tall, wide), jnp.float32),
            pltpu.VMEM((2, tall, wide), jnp.float32),
            pltpu.VMEM((2, size // LANES, size, LANES), jnp.float32),
            pltpu.SemaphoreType.DMA((9,)),
        ],
        compiler_params=pltpu.CompilerParams(vmem_limit_bytes=28 * MIB),
        name="patches",
    )(
        counts,
        rows,
        cols,
        *place_of,
        *pieces,
        probe,
        amplitude,
        *(jnp.asarray(table) for table in dft_tables(size)),
    )


def haar_kernel(
    core_of,
    odd_of,
    inner,
    first,
    second,
    near_mid,
    far_mid,
    far_top,
    far_bottom,
    out,
    *scratch,
):
    height, width = inner.shape[1:]
    margin = first.shape[1]
    core, odd = core_of[0], odd_of[0]
    levels = [scratch[level] for level in range(LEVELS)]
    details = [scratch[LEVELS + level] for level in range(LEVELS - 1)]
    columns = width // LANES
    work = levels[0]
    near = (1 - core) * (columns - 1)
    far = core * (columns - 1)
    first_rows = pl.ds(pl.multiple_of((1 - odd) * (height - margin), margin), margin)
    second_rows = pl.ds(pl.multiple_of(odd * (height - margin), margin), margin)
    for part in range(2):
        for column in range(columns):
            piece = part, slice(None), pl.ds(column * LANES, LANES)
            work[part, column] = inner[piece]
            work[part, column, first_rows] -= STEP_OBJECT * first[piece]
            work[part, column, second_rows] -= STEP_OBJECT * second[piece]
        work[part, near] -= STEP_OBJECT * near_mid[part]
        corners = jnp.concatenate([far_top[part], far_bottom[part]], axis=0)
        work[part, far] -= STEP_OBJECT * (far_mid[part] + corners)

    lane = lax.broadcasted_iota(jnp.int32, (TILE, LANES), 1)

    def each(function, *parts):
        return [[function(*pair) for pair in zip(*rows)] for rows in zip(*parts)]

    def level_steps(level):
        stride = 1 << level
        active = lane % stride == 0
        second = lane % (2 * stride) == stride
        keep = jnp.where(active, jnp.where(second, -0.5, 0.5), 1.0).astype(jnp.float32)
        swap = jnp.where(active, 0.5, 0.0).astype(jnp.float32)

        def lane_step(values):
            after = each(lambda value: pltpu.roll(value, LANES - stride, 1), values)
            before = each(lambda value: pltpu.roll(value, stride, 1), values)
            return each(
                lambda value, high, low: value * keep + jnp.where(second, low, high) * swap,
                values,
                after,
                before,
            )

        def row_step(first, other):
            if level == 0:
                return each(jnp.add, first, other), each(jnp.subtract, first, other)
            return (
                each(lambda a, b: jnp.where(active, a + b, a), first, other),
                each(lambda a, b: jnp.where(active, a - b, b), first, other),
            )

        return lane_step, row_step

    def shrink(values, kept=None):
        factors = []
        for real, imag in zip(*values):
            power = real * real + imag * imag
            factor = jnp.maximum(
                1.0 - THRESHOLD * lax.rsqrt(jnp.maximum(power, THRESHOLD * THRESHOLD)), 0.0
            )
            factors.append(factor if kept is None else jnp.where(kept, 1.0, factor))
        return [[value * factor for value, factor in zip(row, factors)] for row in values]

    def load(ref, start, stride=None):
        where = pl.ds(start, TILE) if stride is None else pl.ds(start, TILE, stride=stride)
        return [[ref[part, column, where, :] for column in range(columns)] for part in range(2)]

    def save(ref, values, start, stride=None):
        where = pl.ds(start, TILE) if stride is None else pl.ds(start, TILE, stride=stride)
        for part in range(2):
            for column in range(columns):
                ref[part, column, where, :] = values[part][column]

    for level in range(LEVELS - 1):
        lane_step, row_step = level_steps(level)

        for index in range(height >> (level + 4)):
            base = index * 2 * TILE
            first = load(levels[level], base, 2)
            other = load(levels[level], base + 1, 2)
            low, high = row_step(first, other)
            save(levels[level + 1], lane_step(low), index * TILE)
            save(details[level], shrink(lane_step(high)), index * TILE)

    lane_step, row_step = level_steps(LEVELS - 1)
    coarsest = lane % (1 << LEVELS) == 0
    for index in range(height >> (LEVELS + 3)):
        base = index * 2 * TILE
        low, high = row_step(load(levels[-1], base, 2), load(levels[-1], base + 1, 2))
        low = lane_step(shrink(lane_step(low), coarsest))
        high = lane_step(shrink(lane_step(high)))
        first, other = row_step(low, high)
        save(levels[-1], first, base, 2)
        save(levels[-1], other, base + 1, 2)

    for level in range(LEVELS - 1)[::-1]:
        lane_step, row_step = level_steps(level)
        for index in range(height >> (level + 4)):
            low = lane_step(load(levels[level + 1], index * TILE))
            high = lane_step(load(details[level], index * TILE))
            first, other = row_step(low, high)
            base = index * 2 * TILE
            save(levels[level], first, base, 2)
            save(levels[level], other, base + 1, 2)
    for part in range(2):
        for column in range(columns):
            out[part, :, pl.ds(column * LANES, LANES)] = work[part, column]


def shrink_object(place_of, *pieces):
    smem = pl.BlockSpec(memory_space=pltpu.SMEM)
    vmem = pl.BlockSpec(memory_space=pltpu.VMEM)
    shape = pieces[0].shape
    sizes = [(2, shape[2] // LANES, shape[1] >> level, LANES) for level in range(LEVELS)]
    return pl.pallas_call(
        haar_kernel,
        out_shape=jax.ShapeDtypeStruct(shape, jnp.float32),
        in_specs=[smem] * 2 + [vmem] * len(pieces),
        out_specs=vmem,
        scratch_shapes=[pltpu.VMEM(size, jnp.float32) for size in sizes + sizes[1:]],
        compiler_params=pltpu.CompilerParams(vmem_limit_bytes=16 * MIB),
        name="haar",
    )(*place_of, *pieces)


def join_kernel(core_of, first, second, given, kept, first_out, second_out, shares):
    margin = first.shape[1]
    width = first.shape[2]
    near = pl.ds(pl.multiple_of((1 - core_of[0]) * (width - LANES), LANES), LANES)
    first_out[...] = first[...]
    second_out[...] = second[...]
    first_out[:, :, near] += given[:, :margin]
    second_out[:, :, near] += given[:, margin : 2 * margin]
    shares[...] = (kept[...] + given[:, 2 * margin :]).reshape(shares.shape)


def joined(core_of, first, second, given, kept, parts):
    smem = pl.BlockSpec(memory_space=pltpu.SMEM)
    vmem = pl.BlockSpec(memory_space=pltpu.VMEM)
    shapes = [first.shape, second.shape, (parts, kept.size // (parts * LANES), LANES)]
    return pl.pallas_call(
        join_kernel,
        out_shape=tuple(jax.ShapeDtypeStruct(shape, jnp.float32) for shape in shapes),
        in_specs=[smem] + [vmem] * 4,
        out_specs=[vmem] * 3,
        compiler_params=pltpu.CompilerParams(vmem_limit_bytes=8 * MIB),
        name="joined",
    )(core_of, first, second, given, kept)


def added(parts):
    total = parts[0]
    for index in range(1, parts.shape[0]):
        total = total + parts[index]
    return total


def tile_kernel(parts, tile, out):
    scale = PROBE_STEP / (PATCHES * DEVICES)
    out[...] = jnp.broadcast_to((tile[...] - scale * added(parts))[None], out.shape)


def summed(parts, copies, tile):
    vmem = pl.BlockSpec(memory_space=pltpu.VMEM)
    return pl.pallas_call(
        tile_kernel,
        out_shape=jax.ShapeDtypeStruct((copies,) + parts.shape[1:], jnp.float32),
        in_specs=[vmem] * 2,
        out_specs=vmem,
        compiler_params=pltpu.CompilerParams(vmem_limit_bytes=4 * MIB),
        name="summed",
    )(parts, tile)


def probe_kernel(tiles, out):
    rows = tiles.shape[2]
    chunks = out.shape[1] // rows
    for part in range(2):
        for half in range(2):
            value = tiles[pl.ds(part * chunks, chunks), half]
            out[part, :, pl.ds(half * LANES, LANES)] = value.reshape(out.shape[1], LANES)


def laid_out(tiles, shape):
    vmem = pl.BlockSpec(memory_space=pltpu.VMEM)
    return pl.pallas_call(
        probe_kernel,
        out_shape=jax.ShapeDtypeStruct(shape, jnp.float32),
        in_specs=[vmem],
        out_specs=vmem,
        compiler_params=pltpu.CompilerParams(vmem_limit_bytes=4 * MIB),
        name="laid_out",
    )(tiles)


def permuted(value, move):
    rows, cols = lax.axis_size(ROW), lax.axis_size(COL)
    pairs = []
    for source in range(rows * cols):
        row, col = move(source // cols, source % cols)
        if 0 <= row < rows and 0 <= col < cols:
            pairs.append((source, row * cols + col))
    return lax.ppermute(value, AXES, pairs)


def up_by(step):
    return lambda row, col: (row + step, col)


def near_to(row, col):
    return row, col ^ 1


def far_to(step):
    return lambda row, col: (row + step, col - 1 if col % 2 == 0 else col + 1)


def pair_to(first):
    return lambda row, col: (row + (1 if (row % 2 == 0) == first else -1), col)


def on_device(object_now, object_prev, probe, amplitudes, pos_row, pos_col, counts):
    centre = object_now + MOMENTUM * (object_now - object_prev)
    margin = probe.shape[1] // 2
    height, width = centre.shape[1:]
    slots = amplitudes.shape[2]
    core = lax.axis_index("core")
    place_of = core.reshape(1), lax.axis_index("xh").reshape(1)

    def sides(value):
        first, last = value[:, :, :margin], value[:, :, width - margin :]
        return jnp.where(core == 0, last, first), jnp.where(core == 0, first, last)

    near, far = sides(centre)
    top = permuted(centre[:, height - margin :], up_by(1))
    bottom = permuted(centre[:, :margin], up_by(-1))
    far_top = permuted(far[:, height - margin :], far_to(1))
    far_bottom = permuted(far[:, :margin], far_to(-1))
    far_mid = permuted(far, far_to(0))
    near_mid = permuted(near, near_to)
    near_corner, far_top, far_bottom, far_mid = lax.optimization_barrier(
        (
            jnp.concatenate([sides(top)[0], sides(bottom)[0]], axis=1),
            far_top,
            far_bottom,
            far_mid,
        )
    )
    near_corner = permuted(near_corner, near_to)
    (
        inner,
        first,
        second,
        near_mid,
        far_mid,
        given,
        far_top,
        far_bottom,
        probe_kept,
    ) = patches(
        counts.reshape(1),
        pos_row.reshape(slots),
        pos_col.reshape(slots),
        place_of,
        (centre, top, bottom, near_mid, far_mid, near_corner, far_top, far_bottom),
        probe,
        ordered_amplitude(amplitudes[0, 0]),
    )
    given = permuted(given, near_to)
    first, second, shares = joined(
        place_of[0], first, second, given, probe_kept, lax.axis_size(CHIPS)
    )
    first, second, far_top, far_bottom, far_mid, near_mid, shares = lax.optimization_barrier(
        (first, second, far_top, far_bottom, far_mid, near_mid, shares)
    )
    first = permuted(first, pair_to(True))
    first, second = lax.optimization_barrier((first, second))
    second = permuted(second, pair_to(False))
    far_below = permuted(far_top, far_to(-1))
    far_above = permuted(far_bottom, far_to(1))
    far_mid, far_below, far_above = lax.optimization_barrier((far_mid, far_below, far_above))
    far_mid = permuted(far_mid, far_to(0))
    near_mid, first, second, far_mid = lax.optimization_barrier(
        (near_mid, first, second, far_mid)
    )
    near_mid = permuted(near_mid, near_to)
    shares = lax.all_to_all(shares, CHIPS, 0, 0, tiled=True)
    columns = [probe[:, :, LANES * index : LANES * (index + 1)] for index in range(2)]
    tile = jnp.where(core == 0, *columns).reshape(shares.shape)
    tile = lax.dynamic_index_in_dim(tile, lax.axis_index(CHIPS), keepdims=False)
    tiles = summed(shares, lax.axis_size(AXES), tile)
    tiles = lax.all_to_all(tiles, AXES, 0, 0, tiled=True)
    object_new = shrink_object(
        place_of, inner, first, second, near_mid, far_mid, far_above, far_below
    )
    object_new, tiles = lax.optimization_barrier((object_new, tiles))
    probe_new = laid_out(tiles.reshape((-1, 2) + tile.shape), probe.shape)
    return object_new, probe_new


def solution(mesh):
    fine = jax.sharding.Mesh(mesh.devices.reshape(4, 2, 4, 2, 2), AXES)
    in_specs = (
        P(None, ROW, COL),
        P(None, ROW, COL),
        P(),
        P(ROW, COL, None, None, None),
        P(ROW, COL, None),
        P(ROW, COL, None),
        P(ROW, COL),
    )
    out_specs = (P(None, ROW, COL), P())
    return jax.shard_map(
        on_device, mesh=fine, in_specs=in_specs, out_specs=out_specs, check_vma=False
    )
```

```python
import math

import jax
import jax.numpy as jnp
import ml_dtypes
import numpy as np
from jax import lax
from jax.experimental import pallas as pl
from jax.experimental.pallas import tpu as pltpu
from jax.sharding import PartitionSpec as P

LEVELS = 4
MOMENTUM = 0.6
STEP_OBJECT = 0.5
PROBE_STEP = 2.0
THRESHOLD = 0.3
FLOOR = 0.5

ROW = ("z", "xh")
COL = ("y", "xl", "core")
AXES = ROW + COL
CHIPS = ROW + COL[:2]
LANES = 128
PATCHES = 4
DEVICES = 128
TILE = 8
MIB = 1024 * 1024


def split_table(table):
    high = table.astype(ml_dtypes.bfloat16)
    low = (table - high.astype(np.float64)).astype(ml_dtypes.bfloat16)
    return high, low


def dft_tables(length):
    half = length // 2
    points = np.arange(half)
    angles = (points[:, None] * points[None, :] % half) * (-2.0 * math.pi / half)
    real = np.cos(angles) / math.sqrt(length)
    imag = np.sin(angles) / math.sqrt(length)
    left_high, left_low = split_table(np.block([[real, -imag], [imag, real]]))
    right_high, right_low = split_table(np.block([[real, imag], [-imag, real]]))
    turn = points * (-2.0 * math.pi / length)
    twiddle = np.stack([np.cos(turn), np.sin(turn)]).astype(np.float32)
    return (
        np.concatenate([left_high, left_high, left_low], axis=1),
        np.concatenate([right_high, right_high, right_low], axis=0),
        np.concatenate(
            [np.repeat(twiddle[:, :, None], LANES, axis=2), np.repeat(twiddle[:, None, :], half, axis=1)]
        ),
    )


def split_value(value):
    high = value.astype(jnp.bfloat16)
    low = (value - high.astype(jnp.float32)).astype(jnp.bfloat16)
    return high, low


def times(real, imag, twiddle):
    cosine, sine = twiddle
    return real * cosine - imag * sine, real * sine + imag * cosine


def left_product(blocks, table):
    half = blocks[0][0].shape[0]
    width = blocks[0][0].shape[1]
    value = jnp.concatenate(
        [jnp.concatenate([real, imag], axis=0) for real, imag in blocks], axis=1
    )
    high, low = split_value(value)
    out = jnp.dot(
        table[...],
        jnp.concatenate([high, low, high], axis=0),
        preferred_element_type=jnp.float32,
    )
    return [
        (out[:half, index * width : (index + 1) * width], out[half:, index * width : (index + 1) * width])
        for index in range(len(blocks))
    ]


def right_product(blocks, table):
    half = blocks[0][0].shape[1]
    value = jnp.concatenate(
        [jnp.concatenate([real, imag], axis=1) for real, imag in blocks], axis=0
    )
    high, low = split_value(value)
    out = jnp.dot(
        jnp.concatenate([high, low, high], axis=1),
        table[...],
        preferred_element_type=jnp.float32,
    )
    return [
        (out[index * half : (index + 1) * half, :half], out[index * half : (index + 1) * half, half:])
        for index in range(len(blocks))
    ]


def forward(real, imag, left_table, right_table, row_twiddle, lane_twiddle):
    half = real.shape[0] // 2
    wide_twiddle = [jnp.concatenate([part, part], axis=1) for part in row_twiddle]
    total = (real[:half] + real[half:], imag[:half] + imag[half:])
    gap = times(real[:half] - real[half:], imag[:half] - imag[half:], wide_twiddle)
    blocks = []
    for real, imag in left_product([total, gap], left_table):
        blocks.append((real[:, :half] + real[:, half:], imag[:, :half] + imag[:, half:]))
        blocks.append(
            times(real[:, :half] - real[:, half:], imag[:, :half] - imag[:, half:], lane_twiddle)
        )
    return right_product(blocks, right_table)


def backward(blocks, left_table, right_table, row_twiddle, lane_twiddle):
    blocks = right_product(blocks, right_table)
    wide_twiddle = [jnp.concatenate([part, part], axis=1) for part in row_twiddle]
    joined = []
    for parity in range(2):
        even_real, even_imag = blocks[2 * parity]
        odd_real, odd_imag = times(*blocks[2 * parity + 1], lane_twiddle)
        joined.append(
            (
                jnp.concatenate([even_real + odd_real, even_real - odd_real], axis=1),
                jnp.concatenate([even_imag + odd_imag, even_imag - odd_imag], axis=1),
            )
        )
    (even_real, even_imag), odd = left_product(joined, left_table)
    odd_real, odd_imag = times(*odd, wide_twiddle)
    return (
        jnp.concatenate([even_real + odd_real, even_real - odd_real], axis=0),
        jnp.concatenate([even_imag + odd_imag, even_imag - odd_imag], axis=0),
    )


def order_table(size):
    half = size // 2
    table = np.zeros((size, size), np.float32)
    table[2 * np.arange(half), np.arange(half)] = 1
    table[2 * np.arange(half) + 1, half + np.arange(half)] = 1
    return np.concatenate([table] * 3, axis=0).astype(ml_dtypes.bfloat16)


def order_amplitude(slot, amplitude, table, sorted_lanes, ordered):
    size = amplitude.shape[1]
    half = size // 2
    value = amplitude[slot]
    high = value.astype(jnp.bfloat16)
    middle, low = split_value(value - high.astype(jnp.float32))
    turned = jnp.dot(
        jnp.concatenate([high, middle, low], axis=1),
        table[...],
        preferred_element_type=jnp.float32,
    )
    for index in range(2):
        sorted_lanes[index] = turned[:, index * half : (index + 1) * half]
        for parity in range(2):
            ordered[slot, 2 * parity + index] = sorted_lanes[
                index, pl.ds(parity, half, stride=2), :
            ]


def patch_kernel(
    counts,
    rows,
    cols,
    core_of,
    odd_of,
    centre,
    top,
    bottom,
    near_mid,
    far_mid,
    near_corner,
    far_top,
    far_bottom,
    amplitude_in,
    probe,
    order,
    left_table,
    right_table,
    twiddle_table,
    inner_out,
    first_out,
    second_out,
    near_mid_out,
    far_mid_out,
    given_out,
    far_top_out,
    far_bottom_out,
    probe_out,
    extended,
    gradient,
    probe_sum,
    measured,
    sorted_lanes,
    amplitude,
    sems,
):
    size = probe.shape[1]
    margin = size // 2
    height, width = centre.shape[1:]
    inner = pl.ds(margin, width)
    core, odd = core_of[0], odd_of[0]
    near = pl.ds(pl.multiple_of((1 - core) * (margin + width), LANES), margin)
    far = pl.ds(pl.multiple_of(core * (margin + width), LANES), margin)
    first = pl.ds(pl.multiple_of((1 - odd) * (margin + height), margin), margin)
    second = pl.ds(pl.multiple_of(odd * (margin + height), margin), margin)
    head, middle, tail = pl.ds(0, margin), pl.ds(margin, height), pl.ds(margin + height, margin)
    moves = [
        (centre, extended.at[:, middle, inner]),
        (near_mid, extended.at[:, middle, near]),
        (far_mid, extended.at[:, middle, far]),
        (top, extended.at[:, head, inner]),
        (bottom, extended.at[:, tail, inner]),
        (far_top, extended.at[:, head, far]),
        (far_bottom, extended.at[:, tail, far]),
        (near_corner.at[:, head, :], extended.at[:, head, near]),
        (near_corner.at[:, pl.ds(margin, margin), :], extended.at[:, tail, near]),
    ]
    copies = [
        pltpu.make_async_copy(source, target, sems.at[index])
        for index, (source, target) in enumerate(moves)
    ]
    measured_copy = pltpu.make_async_copy(amplitude_in, measured, sems.at[len(moves)])
    measured_copy.start()
    for copy in copies:
        copy.start()
    gradient[...] = jnp.zeros_like(gradient)
    probe_sum[...] = jnp.zeros_like(probe_sum)
    measured_copy.wait()

    def order_slot(slot, carry):
        order_amplitude(slot, measured, order, sorted_lanes, amplitude)
        return carry

    lax.fori_loop(0, counts[0], order_slot, 0)
    for copy in copies:
        copy.wait()
    tile = (1, TILE, LANES)
    lane = lax.broadcasted_iota(jnp.int32, tile, 2)
    sublane = lax.broadcasted_iota(jnp.int32, tile, 1)
    tiles = size // TILE
    pieces = size // LANES

    tables = (
        left_table,
        right_table,
        (twiddle_table[0], twiddle_table[1]),
        (twiddle_table[2], twiddle_table[3]),
    )

    def place(slot):
        row_shift = lax.rem(rows[slot], TILE)
        col_shift = lax.rem(cols[slot], LANES)
        row = pl.multiple_of(rows[slot] - row_shift, TILE)
        col = pl.multiple_of(cols[slot] - col_shift, LANES)
        areas = [
            (pl.ds(row, size + TILE), pl.ds(col + LANES * piece, LANES))
            for piece in range(pieces + 1)
        ]
        return row_shift, col_shift, areas

    def window(part, row_shift, col_shift, areas):
        columns = [
            pltpu.roll(
                extended[(part,) + area].reshape(tiles + 1, TILE, LANES),
                lax.rem(LANES - col_shift, LANES),
                2,
            )
            for area in areas
        ]
        result = []
        for piece in range(pieces):
            value = jnp.where(lane < LANES - col_shift, columns[piece], columns[piece + 1])
            value = pltpu.roll(value, lax.rem(TILE - row_shift, TILE), 1)
            value = jnp.where(sublane < TILE - row_shift, value[:tiles], value[1:])
            result.append(value.reshape(size, LANES))
        return jnp.concatenate(result, axis=1)

    def add_term(part, term, row_shift, col_shift, areas):
        columns = []
        ended = jnp.zeros(tile, jnp.float32)
        for piece in range(pieces):
            value = term[:, LANES * piece : LANES * (piece + 1)].reshape(tiles, TILE, LANES)
            value = pltpu.roll(value, row_shift, 1)
            value = jnp.where(
                sublane >= row_shift,
                jnp.concatenate([value, ended], axis=0),
                jnp.concatenate([ended, value], axis=0),
            )
            columns.append(pltpu.roll(value, col_shift, 2))
        ended = jnp.zeros_like(columns[0])
        columns = [ended] + columns + [ended]
        for piece, area in enumerate(areas):
            block = jnp.where(lane >= col_shift, columns[piece + 1], columns[piece])
            gradient[(part,) + area] += block.reshape(size + TILE, LANES)

    def some_patches(slots):
        places = [place(slot) for slot in slots]
        windows = [[window(part, *where) for part in range(2)] for where in places]
        probe_real = probe[0]
        probe_imag = probe[1]
        far_fields = [
            forward(
                probe_real * real - probe_imag * imag, probe_real * imag + probe_imag * real, *tables
            )
            for real, imag in windows
        ]
        residuals = []
        for slot, far_field in zip(slots, far_fields):
            residual = []
            for index, (real, imag) in enumerate(far_field):
                power = real * real + imag * imag
                remain = 1.0 - amplitude[slot, index] * lax.rsqrt(
                    jnp.maximum(power, FLOOR * FLOOR)
                )
                residual.append((real * remain, -imag * remain))
            residuals.append(residual)
        backs = [backward(residual, *tables) for residual in residuals]
        probe_terms = [0.0, 0.0]
        for where, (window_real, window_imag), (back_real, back_imag) in zip(places, windows, backs):
            back_imag = -back_imag
            probe_terms[0] += window_real * back_real + window_imag * back_imag
            probe_terms[1] += window_real * back_imag - window_imag * back_real
            add_term(0, probe_real * back_real + probe_imag * back_imag, *where)
            add_term(1, probe_real * back_imag - probe_imag * back_real, *where)
        for part, term in enumerate(probe_terms):
            for piece in range(pieces):
                probe_sum[part, piece] += term[:, LANES * piece : LANES * (piece + 1)]

    def two_patches(index, carry):
        some_patches([2 * index, 2 * index + 1])
        return carry

    count = counts[0]
    lax.fori_loop(0, count // 2, two_patches, 0)

    @pl.when(count % 2 == 1)
    def _():
        some_patches([count - 1])

    gradient[:, middle, inner] = (
        extended[:, middle, inner] - STEP_OBJECT * gradient[:, middle, inner]
    )
    inner_copy = pltpu.make_async_copy(gradient.at[:, middle, inner], inner_out, sems.at[0])
    inner_copy.start()
    given_out[:, :margin] = gradient[:, first, near]
    given_out[:, margin : 2 * margin] = gradient[:, second, near]
    for part in range(2):
        given_out[part, 2 * margin :] = probe_sum[part, 1 - core]
        probe_out[part] = probe_sum[part, core]
    first_out[...] = gradient[:, first, inner]
    second_out[...] = gradient[:, second, inner]
    near_mid_out[...] = gradient[:, middle, near]
    far_mid_out[...] = gradient[:, middle, far]
    far_top_out[...] = gradient[:, head, far]
    far_bottom_out[...] = gradient[:, tail, far]
    inner_copy.wait()


def patches(counts, rows, cols, place_of, pieces, probe, amplitude):
    size = probe.shape[1]
    margin = size // 2
    height, width = pieces[0].shape[1:]
    tall, wide = height + size, width + size
    smem = pl.BlockSpec(memory_space=pltpu.SMEM)
    vmem = pl.BlockSpec(memory_space=pltpu.VMEM)
    anywhere = pl.BlockSpec(memory_space=pl.ANY)
    shapes = [
        (height, width),
        (margin, width),
        (margin, width),
        (height, margin),
        (height, margin),
        (2 * margin + size, margin),
        (margin, margin),
        (margin, margin),
        (size, LANES),
    ]
    return pl.pallas_call(
        patch_kernel,
        out_shape=(pltpu.HBM((2,) + shapes[0], jnp.float32),)
        + tuple(jax.ShapeDtypeStruct((2,) + shape, jnp.float32) for shape in shapes[1:]),
        in_specs=[smem] * 5 + [anywhere] * 9 + [vmem] * 5,
        out_specs=[anywhere] + [vmem] * 8,
        scratch_shapes=[
            pltpu.VMEM((2, tall, wide), jnp.float32),
            pltpu.VMEM((2, tall, wide), jnp.float32),
            pltpu.VMEM((2, size // LANES, size, LANES), jnp.float32),
            pltpu.VMEM(amplitude.shape, jnp.float32),
            pltpu.VMEM((2, size, size // 2), jnp.float32),
            pltpu.VMEM((amplitude.shape[0], 4, size // 2, size // 2), jnp.float32),
            pltpu.SemaphoreType.DMA((10,)),
        ],
        compiler_params=pltpu.CompilerParams(vmem_limit_bytes=28 * MIB),
        name="patches",
    )(
        counts,
        rows,
        cols,
        *place_of,
        *pieces,
        amplitude,
        probe,
        jnp.asarray(order_table(size)),
        *(jnp.asarray(table) for table in dft_tables(size)),
    )


def haar_kernel(
    core_of,
    odd_of,
    inner,
    first,
    second,
    near_mid,
    far_mid,
    far_top,
    far_bottom,
    out,
    *scratch,
):
    height, width = inner.shape[1:]
    margin = first.shape[1]
    core, odd = core_of[0], odd_of[0]
    levels = [scratch[level] for level in range(LEVELS)]
    details = [scratch[LEVELS + level] for level in range(LEVELS - 1)]
    columns = width // LANES
    work = levels[0]
    near = (1 - core) * (columns - 1)
    far = core * (columns - 1)
    first_rows = pl.ds(pl.multiple_of((1 - odd) * (height - margin), margin), margin)
    second_rows = pl.ds(pl.multiple_of(odd * (height - margin), margin), margin)
    for part in range(2):
        for column in range(columns):
            piece = part, slice(None), pl.ds(column * LANES, LANES)
            work[part, column] = inner[piece]
            work[part, column, first_rows] -= STEP_OBJECT * first[piece]
            work[part, column, second_rows] -= STEP_OBJECT * second[piece]
        work[part, near] -= STEP_OBJECT * near_mid[part]
        corners = jnp.concatenate([far_top[part], far_bottom[part]], axis=0)
        work[part, far] -= STEP_OBJECT * (far_mid[part] + corners)

    lane = lax.broadcasted_iota(jnp.int32, (TILE, LANES), 1)

    def each(function, *parts):
        return [[function(*pair) for pair in zip(*rows)] for rows in zip(*parts)]

    def level_steps(level):
        stride = 1 << level
        active = lane % stride == 0
        second = lane % (2 * stride) == stride
        keep = jnp.where(active, jnp.where(second, -0.5, 0.5), 1.0).astype(jnp.float32)
        swap = jnp.where(active, 0.5, 0.0).astype(jnp.float32)

        def lane_step(values):
            after = each(lambda value: pltpu.roll(value, LANES - stride, 1), values)
            before = each(lambda value: pltpu.roll(value, stride, 1), values)
            return each(
                lambda value, high, low: value * keep + jnp.where(second, low, high) * swap,
                values,
                after,
                before,
            )

        def row_step(first, other):
            if level == 0:
                return each(jnp.add, first, other), each(jnp.subtract, first, other)
            return (
                each(lambda a, b: jnp.where(active, a + b, a), first, other),
                each(lambda a, b: jnp.where(active, a - b, b), first, other),
            )

        return lane_step, row_step

    def shrink(values, kept=None):
        factors = []
        for real, imag in zip(*values):
            power = real * real + imag * imag
            factor = jnp.maximum(
                1.0 - THRESHOLD * lax.rsqrt(jnp.maximum(power, THRESHOLD * THRESHOLD)), 0.0
            )
            factors.append(factor if kept is None else jnp.where(kept, 1.0, factor))
        return [[value * factor for value, factor in zip(row, factors)] for row in values]

    def load(ref, start, stride=None):
        where = pl.ds(start, TILE) if stride is None else pl.ds(start, TILE, stride=stride)
        return [[ref[part, column, where, :] for column in range(columns)] for part in range(2)]

    def save(ref, values, start, stride=None):
        where = pl.ds(start, TILE) if stride is None else pl.ds(start, TILE, stride=stride)
        for part in range(2):
            for column in range(columns):
                ref[part, column, where, :] = values[part][column]

    for level in range(LEVELS - 1):
        lane_step, row_step = level_steps(level)

        for index in range(height >> (level + 4)):
            base = index * 2 * TILE
            first = load(levels[level], base, 2)
            other = load(levels[level], base + 1, 2)
            low, high = row_step(first, other)
            save(levels[level + 1], lane_step(low), index * TILE)
            save(details[level], shrink(lane_step(high)), index * TILE)

    lane_step, row_step = level_steps(LEVELS - 1)
    coarsest = lane % (1 << LEVELS) == 0
    for index in range(height >> (LEVELS + 3)):
        base = index * 2 * TILE
        low, high = row_step(load(levels[-1], base, 2), load(levels[-1], base + 1, 2))
        low = lane_step(shrink(lane_step(low), coarsest))
        high = lane_step(shrink(lane_step(high)))
        first, other = row_step(low, high)
        save(levels[-1], first, base, 2)
        save(levels[-1], other, base + 1, 2)

    for level in range(LEVELS - 1)[::-1]:
        lane_step, row_step = level_steps(level)
        for index in range(height >> (level + 4)):
            low = lane_step(load(levels[level + 1], index * TILE))
            high = lane_step(load(details[level], index * TILE))
            first, other = row_step(low, high)
            base = index * 2 * TILE
            save(levels[level], first, base, 2)
            save(levels[level], other, base + 1, 2)
    for part in range(2):
        for column in range(columns):
            out[part, :, pl.ds(column * LANES, LANES)] = work[part, column]


def shrink_object(place_of, *pieces):
    smem = pl.BlockSpec(memory_space=pltpu.SMEM)
    vmem = pl.BlockSpec(memory_space=pltpu.VMEM)
    shape = pieces[0].shape
    sizes = [(2, shape[2] // LANES, shape[1] >> level, LANES) for level in range(LEVELS)]
    return pl.pallas_call(
        haar_kernel,
        out_shape=jax.ShapeDtypeStruct(shape, jnp.float32),
        in_specs=[smem] * 2 + [vmem] * len(pieces),
        out_specs=vmem,
        scratch_shapes=[pltpu.VMEM(size, jnp.float32) for size in sizes + sizes[1:]],
        compiler_params=pltpu.CompilerParams(vmem_limit_bytes=16 * MIB),
        name="haar",
    )(*place_of, *pieces)


def join_kernel(core_of, first, second, given, kept, first_out, second_out, shares):
    margin = first.shape[1]
    width = first.shape[2]
    near = pl.ds(pl.multiple_of((1 - core_of[0]) * (width - LANES), LANES), LANES)
    first_out[...] = first[...]
    second_out[...] = second[...]
    first_out[:, :, near] += given[:, :margin]
    second_out[:, :, near] += given[:, margin : 2 * margin]
    shares[...] = (kept[...] + given[:, 2 * margin :]).reshape(shares.shape)


def joined(core_of, first, second, given, kept, parts):
    smem = pl.BlockSpec(memory_space=pltpu.SMEM)
    vmem = pl.BlockSpec(memory_space=pltpu.VMEM)
    shapes = [first.shape, second.shape, (parts, kept.size // (parts * LANES), LANES)]
    return pl.pallas_call(
        join_kernel,
        out_shape=tuple(jax.ShapeDtypeStruct(shape, jnp.float32) for shape in shapes),
        in_specs=[smem] + [vmem] * 4,
        out_specs=[vmem] * 3,
        compiler_params=pltpu.CompilerParams(vmem_limit_bytes=8 * MIB),
        name="joined",
    )(core_of, first, second, given, kept)


def added(parts):
    total = parts[0]
    for index in range(1, parts.shape[0]):
        total = total + parts[index]
    return total


def tile_kernel(parts, tile, out):
    scale = PROBE_STEP / (PATCHES * DEVICES)
    out[...] = jnp.broadcast_to((tile[...] - scale * added(parts))[None], out.shape)


def summed(parts, copies, tile):
    vmem = pl.BlockSpec(memory_space=pltpu.VMEM)
    return pl.pallas_call(
        tile_kernel,
        out_shape=jax.ShapeDtypeStruct((copies,) + parts.shape[1:], jnp.float32),
        in_specs=[vmem] * 2,
        out_specs=vmem,
        compiler_params=pltpu.CompilerParams(vmem_limit_bytes=4 * MIB),
        name="summed",
    )(parts, tile)


def probe_kernel(tiles, out):
    rows = tiles.shape[2]
    chunks = out.shape[1] // rows
    for part in range(2):
        for half in range(2):
            value = tiles[pl.ds(part * chunks, chunks), half]
            out[part, :, pl.ds(half * LANES, LANES)] = value.reshape(out.shape[1], LANES)


def laid_out(tiles, shape):
    vmem = pl.BlockSpec(memory_space=pltpu.VMEM)
    return pl.pallas_call(
        probe_kernel,
        out_shape=jax.ShapeDtypeStruct(shape, jnp.float32),
        in_specs=[vmem],
        out_specs=vmem,
        compiler_params=pltpu.CompilerParams(vmem_limit_bytes=4 * MIB),
        name="laid_out",
    )(tiles)


def permuted(value, move):
    rows, cols = lax.axis_size(ROW), lax.axis_size(COL)
    pairs = []
    for source in range(rows * cols):
        row, col = move(source // cols, source % cols)
        if 0 <= row < rows and 0 <= col < cols:
            pairs.append((source, row * cols + col))
    return lax.ppermute(value, AXES, pairs)


def up_by(step):
    return lambda row, col: (row + step, col)


def near_to(row, col):
    return row, col ^ 1


def far_to(step):
    return lambda row, col: (row + step, col - 1 if col % 2 == 0 else col + 1)


def pair_to(first):
    return lambda row, col: (row + (1 if (row % 2 == 0) == first else -1), col)


def on_device(object_now, object_prev, probe, amplitudes, pos_row, pos_col, counts):
    centre = object_now + MOMENTUM * (object_now - object_prev)
    margin = probe.shape[1] // 2
    height, width = centre.shape[1:]
    slots = amplitudes.shape[2]
    core = lax.axis_index("core")
    place_of = core.reshape(1), lax.axis_index("xh").reshape(1)

    def sides(value):
        first, last = value[:, :, :margin], value[:, :, width - margin :]
        return jnp.where(core == 0, last, first), jnp.where(core == 0, first, last)

    near, far = sides(centre)
    top = permuted(centre[:, height - margin :], up_by(1))
    bottom = permuted(centre[:, :margin], up_by(-1))
    far_top = permuted(far[:, height - margin :], far_to(1))
    far_bottom = permuted(far[:, :margin], far_to(-1))
    far_mid = permuted(far, far_to(0))
    near_mid = permuted(near, near_to)
    near_corner, far_top, far_bottom, far_mid = lax.optimization_barrier(
        (
            jnp.concatenate([sides(top)[0], sides(bottom)[0]], axis=1),
            far_top,
            far_bottom,
            far_mid,
        )
    )
    near_corner = permuted(near_corner, near_to)
    (
        inner,
        first,
        second,
        near_mid,
        far_mid,
        given,
        far_top,
        far_bottom,
        probe_kept,
    ) = patches(
        counts.reshape(1),
        pos_row.reshape(slots),
        pos_col.reshape(slots),
        place_of,
        (centre, top, bottom, near_mid, far_mid, near_corner, far_top, far_bottom),
        probe,
        amplitudes[0, 0],
    )
    given = permuted(given, near_to)
    first, second, shares = joined(
        place_of[0], first, second, given, probe_kept, lax.axis_size(CHIPS)
    )
    first, second, far_top, far_bottom, far_mid, near_mid, shares = lax.optimization_barrier(
        (first, second, far_top, far_bottom, far_mid, near_mid, shares)
    )
    first = permuted(first, pair_to(True))
    first, second = lax.optimization_barrier((first, second))
    second = permuted(second, pair_to(False))
    far_below = permuted(far_top, far_to(-1))
    far_above = permuted(far_bottom, far_to(1))
    far_mid, far_below, far_above = lax.optimization_barrier((far_mid, far_below, far_above))
    far_mid = permuted(far_mid, far_to(0))
    near_mid, first, second, far_mid = lax.optimization_barrier(
        (near_mid, first, second, far_mid)
    )
    near_mid = permuted(near_mid, near_to)
    shares = lax.all_to_all(shares, CHIPS, 0, 0, tiled=True)
    columns = [probe[:, :, LANES * index : LANES * (index + 1)] for index in range(2)]
    tile = jnp.where(core == 0, *columns).reshape(shares.shape)
    tile = lax.dynamic_index_in_dim(tile, lax.axis_index(CHIPS), keepdims=False)
    tiles = summed(shares, lax.axis_size(AXES), tile)
    tiles = lax.all_to_all(tiles, AXES, 0, 0, tiled=True)
    object_new = shrink_object(
        place_of, inner, first, second, near_mid, far_mid, far_above, far_below
    )
    object_new, tiles = lax.optimization_barrier((object_new, tiles))
    probe_new = laid_out(tiles.reshape((-1, 2) + tile.shape), probe.shape)
    return object_new, probe_new


def solution(mesh):
    fine = jax.sharding.Mesh(mesh.devices.reshape(4, 2, 4, 2, 2), AXES)
    in_specs = (
        P(None, ROW, COL),
        P(None, ROW, COL),
        P(),
        P(ROW, COL, None, None, None),
        P(ROW, COL, None),
        P(ROW, COL, None),
        P(ROW, COL),
    )
    out_specs = (P(None, ROW, COL), P())
    return jax.shard_map(
        on_device, mesh=fine, in_specs=in_specs, out_specs=out_specs, check_vma=False
    )
```

```python
import math

import jax
import jax.numpy as jnp
import ml_dtypes
import numpy as np
from jax import lax
from jax.experimental import pallas as pl
from jax.experimental.pallas import tpu as pltpu
from jax.sharding import PartitionSpec as P

LEVELS = 4
MOMENTUM = 0.6
STEP_OBJECT = 0.5
PROBE_STEP = 2.0
THRESHOLD = 0.3
FLOOR = 0.5

ROW = ("z", "xh")
COL = ("y", "xl", "core")
AXES = ROW + COL
CHIPS = ROW + COL[:2]
LANES = 128
PATCHES = 4
DEVICES = 128
TILE = 8
MIB = 1024 * 1024


def split_table(table):
    high = table.astype(ml_dtypes.bfloat16)
    low = (table - high.astype(np.float64)).astype(ml_dtypes.bfloat16)
    return high, low


def dft_tables(length):
    half = length // 2
    points = np.arange(half)
    angles = (points[:, None] * points[None, :] % half) * (-2.0 * math.pi / half)
    real = np.cos(angles) / math.sqrt(length)
    imag = np.sin(angles) / math.sqrt(length)
    left_high, left_low = split_table(np.block([[real, -imag], [imag, real]]))
    right_high, right_low = split_table(np.block([[real, imag], [-imag, real]]))
    turn = points * (-2.0 * math.pi / length)
    twiddle = np.stack([np.cos(turn), np.sin(turn)]).astype(np.float32)
    return (
        np.concatenate([left_high, left_high, left_low], axis=1),
        np.concatenate([right_high, right_high, right_low], axis=0),
        np.concatenate(
            [np.repeat(twiddle[:, :, None], LANES, axis=2), np.repeat(twiddle[:, None, :], half, axis=1)]
        ),
    )


def split_value(value):
    high = value.astype(jnp.bfloat16)
    low = (value - high.astype(jnp.float32)).astype(jnp.bfloat16)
    return high, low


def times(real, imag, twiddle):
    cosine, sine = twiddle
    return real * cosine - imag * sine, real * sine + imag * cosine


def left_product(blocks, table):
    half = blocks[0][0].shape[0]
    width = blocks[0][0].shape[1]
    value = jnp.concatenate(
        [jnp.concatenate([real, imag], axis=0) for real, imag in blocks], axis=1
    )
    high, low = split_value(value)
    out = jnp.dot(
        table[...],
        jnp.concatenate([high, low, high], axis=0),
        preferred_element_type=jnp.float32,
    )
    return [
        (out[:half, index * width : (index + 1) * width], out[half:, index * width : (index + 1) * width])
        for index in range(len(blocks))
    ]


def right_product(blocks, table):
    half = blocks[0][0].shape[1]
    value = jnp.concatenate(
        [jnp.concatenate([real, imag], axis=1) for real, imag in blocks], axis=0
    )
    high, low = split_value(value)
    out = jnp.dot(
        jnp.concatenate([high, low, high], axis=1),
        table[...],
        preferred_element_type=jnp.float32,
    )
    return [
        (out[index * half : (index + 1) * half, :half], out[index * half : (index + 1) * half, half:])
        for index in range(len(blocks))
    ]


def forward(real, imag, left_table, right_table, row_twiddle, lane_twiddle):
    half = real.shape[0] // 2
    wide_twiddle = [jnp.concatenate([part, part], axis=1) for part in row_twiddle]
    total = (real[:half] + real[half:], imag[:half] + imag[half:])
    gap = times(real[:half] - real[half:], imag[:half] - imag[half:], wide_twiddle)
    blocks = []
    for real, imag in left_product([total, gap], left_table):
        blocks.append((real[:, :half] + real[:, half:], imag[:, :half] + imag[:, half:]))
        blocks.append(
            times(real[:, :half] - real[:, half:], imag[:, :half] - imag[:, half:], lane_twiddle)
        )
    return right_product(blocks, right_table)


def backward(blocks, left_table, right_table, row_twiddle, lane_twiddle):
    blocks = right_product(blocks, right_table)
    wide_twiddle = [jnp.concatenate([part, part], axis=1) for part in row_twiddle]
    joined = []
    for parity in range(2):
        even_real, even_imag = blocks[2 * parity]
        odd_real, odd_imag = times(*blocks[2 * parity + 1], lane_twiddle)
        joined.append(
            (
                jnp.concatenate([even_real + odd_real, even_real - odd_real], axis=1),
                jnp.concatenate([even_imag + odd_imag, even_imag - odd_imag], axis=1),
            )
        )
    (even_real, even_imag), odd = left_product(joined, left_table)
    odd_real, odd_imag = times(*odd, wide_twiddle)
    return (
        jnp.concatenate([even_real + odd_real, even_real - odd_real], axis=0),
        jnp.concatenate([even_imag + odd_imag, even_imag - odd_imag], axis=0),
    )


def order_table(size):
    half = size // 2
    table = np.zeros((size, size), np.float32)
    table[2 * np.arange(half), np.arange(half)] = 1
    table[2 * np.arange(half) + 1, half + np.arange(half)] = 1
    return np.concatenate([table] * 3, axis=0).astype(ml_dtypes.bfloat16)


def order_amplitude(slot, amplitude, table, sorted_lanes, ordered):
    size = amplitude.shape[1]
    half = size // 2
    value = amplitude[slot]
    high = value.astype(jnp.bfloat16)
    middle, low = split_value(value - high.astype(jnp.float32))
    turned = jnp.dot(
        jnp.concatenate([high, middle, low], axis=1),
        table[...],
        preferred_element_type=jnp.float32,
    )
    for index in range(2):
        sorted_lanes[index] = turned[:, index * half : (index + 1) * half]
        for parity in range(2):
            ordered[slot, 2 * parity + index] = sorted_lanes[
                index, pl.ds(parity, half, stride=2), :
            ]


def patch_kernel(
    counts,
    rows,
    cols,
    core_of,
    odd_of,
    centre,
    top,
    bottom,
    near_mid,
    far_mid,
    near_corner,
    far_top,
    far_bottom,
    amplitude_in,
    order_in,
    probe_in,
    left_in,
    right_in,
    twiddle_in,
    inner_out,
    first_out,
    second_out,
    near_mid_out,
    far_mid_out,
    given_out,
    far_top_out,
    far_bottom_out,
    probe_out,
    extended,
    gradient,
    probe_sum,
    measured,
    sorted_lanes,
    amplitude,
    probe,
    order,
    left_table,
    right_table,
    twiddle_table,
    sems,
):
    size = probe.shape[1]
    margin = size // 2
    height, width = centre.shape[1:]
    inner = pl.ds(margin, width)
    core, odd = core_of[0], odd_of[0]
    near = pl.ds(pl.multiple_of((1 - core) * (margin + width), LANES), margin)
    far = pl.ds(pl.multiple_of(core * (margin + width), LANES), margin)
    first = pl.ds(pl.multiple_of((1 - odd) * (margin + height), margin), margin)
    second = pl.ds(pl.multiple_of(odd * (margin + height), margin), margin)
    head, middle, tail = pl.ds(0, margin), pl.ds(margin, height), pl.ds(margin + height, margin)
    moves = [
        (centre, extended.at[:, middle, inner]),
        (near_mid, extended.at[:, middle, near]),
        (far_mid, extended.at[:, middle, far]),
        (top, extended.at[:, head, inner]),
        (bottom, extended.at[:, tail, inner]),
        (far_top, extended.at[:, head, far]),
        (far_bottom, extended.at[:, tail, far]),
        (near_corner.at[:, head, :], extended.at[:, head, near]),
        (near_corner.at[:, pl.ds(margin, margin), :], extended.at[:, tail, near]),
    ]
    copies = [
        pltpu.make_async_copy(source, target, sems.at[index])
        for index, (source, target) in enumerate(moves)
    ]
    constants = [
        (amplitude_in, measured),
        (order_in, order),
        (probe_in, probe),
        (left_in, left_table),
        (right_in, right_table),
        (twiddle_in, twiddle_table),
    ]
    constant_copies = [
        pltpu.make_async_copy(source, target, sems.at[len(moves) + index])
        for index, (source, target) in enumerate(constants)
    ]
    for copy in constant_copies + copies:
        copy.start()
    gradient[...] = jnp.zeros_like(gradient)
    probe_sum[...] = jnp.zeros_like(probe_sum)
    for copy in constant_copies:
        copy.wait()

    def order_slot(slot, carry):
        order_amplitude(slot, measured, order, sorted_lanes, amplitude)
        return carry

    lax.fori_loop(0, counts[0], order_slot, 0)
    for copy in copies:
        copy.wait()
    tile = (1, TILE, LANES)
    lane = lax.broadcasted_iota(jnp.int32, tile, 2)
    sublane = lax.broadcasted_iota(jnp.int32, tile, 1)
    tiles = size // TILE
    pieces = size // LANES

    tables = (
        left_table,
        right_table,
        (twiddle_table[0], twiddle_table[1]),
        (twiddle_table[2], twiddle_table[3]),
    )

    def place(slot):
        row_shift = lax.rem(rows[slot], TILE)
        col_shift = lax.rem(cols[slot], LANES)
        row = pl.multiple_of(rows[slot] - row_shift, TILE)
        col = pl.multiple_of(cols[slot] - col_shift, LANES)
        areas = [
            (pl.ds(row, size + TILE), pl.ds(col + LANES * piece, LANES))
            for piece in range(pieces + 1)
        ]
        return row_shift, col_shift, areas

    def window(part, row_shift, col_shift, areas):
        columns = [
            pltpu.roll(
                extended[(part,) + area].reshape(tiles + 1, TILE, LANES),
                lax.rem(LANES - col_shift, LANES),
                2,
            )
            for area in areas
        ]
        result = []
        for piece in range(pieces):
            value = jnp.where(lane < LANES - col_shift, columns[piece], columns[piece + 1])
            value = pltpu.roll(value, lax.rem(TILE - row_shift, TILE), 1)
            value = jnp.where(sublane < TILE - row_shift, value[:tiles], value[1:])
            result.append(value.reshape(size, LANES))
        return jnp.concatenate(result, axis=1)

    def add_term(part, term, row_shift, col_shift, areas):
        columns = []
        ended = jnp.zeros(tile, jnp.float32)
        for piece in range(pieces):
            value = term[:, LANES * piece : LANES * (piece + 1)].reshape(tiles, TILE, LANES)
            value = pltpu.roll(value, row_shift, 1)
            value = jnp.where(
                sublane >= row_shift,
                jnp.concatenate([value, ended], axis=0),
                jnp.concatenate([ended, value], axis=0),
            )
            columns.append(pltpu.roll(value, col_shift, 2))
        ended = jnp.zeros_like(columns[0])
        columns = [ended] + columns + [ended]
        for piece, area in enumerate(areas):
            block = jnp.where(lane >= col_shift, columns[piece + 1], columns[piece])
            gradient[(part,) + area] += block.reshape(size + TILE, LANES)

    def some_patches(slots):
        places = [place(slot) for slot in slots]
        windows = [[window(part, *where) for part in range(2)] for where in places]
        probe_real = probe[0]
        probe_imag = probe[1]
        far_fields = [
            forward(
                probe_real * real - probe_imag * imag, probe_real * imag + probe_imag * real, *tables
            )
            for real, imag in windows
        ]
        residuals = []
        for slot, far_field in zip(slots, far_fields):
            residual = []
            for index, (real, imag) in enumerate(far_field):
                power = real * real + imag * imag
                remain = 1.0 - amplitude[slot, index] * lax.rsqrt(
                    jnp.maximum(power, FLOOR * FLOOR)
                )
                residual.append((real * remain, -imag * remain))
            residuals.append(residual)
        backs = [backward(residual, *tables) for residual in residuals]
        probe_terms = [0.0, 0.0]
        for where, (window_real, window_imag), (back_real, back_imag) in zip(places, windows, backs):
            back_imag = -back_imag
            probe_terms[0] += window_real * back_real + window_imag * back_imag
            probe_terms[1] += window_real * back_imag - window_imag * back_real
            add_term(0, probe_real * back_real + probe_imag * back_imag, *where)
            add_term(1, probe_real * back_imag - probe_imag * back_real, *where)
        for part, term in enumerate(probe_terms):
            for piece in range(pieces):
                probe_sum[part, piece] += term[:, LANES * piece : LANES * (piece + 1)]

    def two_patches(index, carry):
        some_patches([2 * index, 2 * index + 1])
        return carry

    count = counts[0]
    lax.fori_loop(0, count // 2, two_patches, 0)

    @pl.when(count % 2 == 1)
    def _():
        some_patches([count - 1])

    gradient[:, middle, inner] = (
        extended[:, middle, inner] - STEP_OBJECT * gradient[:, middle, inner]
    )
    inner_copy = pltpu.make_async_copy(gradient.at[:, middle, inner], inner_out, sems.at[0])
    inner_copy.start()
    given_out[:, :margin] = gradient[:, first, near]
    given_out[:, margin : 2 * margin] = gradient[:, second, near]
    for part in range(2):
        given_out[part, 2 * margin :] = probe_sum[part, 1 - core]
        probe_out[part] = probe_sum[part, core]
    first_out[...] = gradient[:, first, inner]
    second_out[...] = gradient[:, second, inner]
    near_mid_out[...] = gradient[:, middle, near]
    far_mid_out[...] = gradient[:, middle, far]
    far_top_out[...] = gradient[:, head, far]
    far_bottom_out[...] = gradient[:, tail, far]
    inner_copy.wait()


def patches(counts, rows, cols, place_of, pieces, probe, amplitude):
    size = probe.shape[1]
    margin = size // 2
    height, width = pieces[0].shape[1:]
    tall, wide = height + size, width + size
    tables = (order_table(size),) + dft_tables(size)
    order, *tables = (jnp.asarray(table) for table in tables)
    constants = (amplitude, order, probe, *tables)
    smem = pl.BlockSpec(memory_space=pltpu.SMEM)
    vmem = pl.BlockSpec(memory_space=pltpu.VMEM)
    anywhere = pl.BlockSpec(memory_space=pl.ANY)
    hbm = pl.BlockSpec(memory_space=pltpu.HBM)
    shapes = [
        (height, width),
        (margin, width),
        (margin, width),
        (height, margin),
        (height, margin),
        (2 * margin + size, margin),
        (margin, margin),
        (margin, margin),
        (size, LANES),
    ]
    return pl.pallas_call(
        patch_kernel,
        out_shape=(pltpu.HBM((2,) + shapes[0], jnp.float32),)
        + tuple(jax.ShapeDtypeStruct((2,) + shape, jnp.float32) for shape in shapes[1:]),
        in_specs=[smem] * 5 + [anywhere] * 8 + [hbm] * 6,
        out_specs=[anywhere] + [vmem] * 8,
        scratch_shapes=[
            pltpu.VMEM((2, tall, wide), jnp.float32),
            pltpu.VMEM((2, tall, wide), jnp.float32),
            pltpu.VMEM((2, size // LANES, size, LANES), jnp.float32),
            pltpu.VMEM(amplitude.shape, jnp.float32),
            pltpu.VMEM((2, size, size // 2), jnp.float32),
            pltpu.VMEM((amplitude.shape[0], 4, size // 2, size // 2), jnp.float32),
            pltpu.VMEM(probe.shape, jnp.float32),
            *(pltpu.VMEM(value.shape, value.dtype) for value in (order, *tables)),
            pltpu.SemaphoreType.DMA((15,)),
        ],
        compiler_params=pltpu.CompilerParams(vmem_limit_bytes=28 * MIB),
        name="patches",
    )(
        counts,
        rows,
        cols,
        *place_of,
        *pieces,
        *(pltpu.with_memory_space_constraint(value, pltpu.HBM) for value in constants),
    )


def haar_kernel(
    core_of,
    odd_of,
    inner,
    first,
    second,
    near_mid,
    far_mid,
    far_top,
    far_bottom,
    out,
    *scratch,
):
    height, width = inner.shape[1:]
    margin = first.shape[1]
    core, odd = core_of[0], odd_of[0]
    levels = [scratch[level] for level in range(LEVELS)]
    details = [scratch[LEVELS + level] for level in range(LEVELS - 1)]
    columns = width // LANES
    work = levels[0]
    near = (1 - core) * (columns - 1)
    far = core * (columns - 1)
    first_rows = pl.ds(pl.multiple_of((1 - odd) * (height - margin), margin), margin)
    second_rows = pl.ds(pl.multiple_of(odd * (height - margin), margin), margin)
    for part in range(2):
        for column in range(columns):
            piece = part, slice(None), pl.ds(column * LANES, LANES)
            work[part, column] = inner[piece]
            work[part, column, first_rows] -= STEP_OBJECT * first[piece]
            work[part, column, second_rows] -= STEP_OBJECT * second[piece]
        work[part, near] -= STEP_OBJECT * near_mid[part]
        corners = jnp.concatenate([far_top[part], far_bottom[part]], axis=0)
        work[part, far] -= STEP_OBJECT * (far_mid[part] + corners)

    lane = lax.broadcasted_iota(jnp.int32, (TILE, LANES), 1)

    def each(function, *parts):
        return [[function(*pair) for pair in zip(*rows)] for rows in zip(*parts)]

    def level_steps(level):
        stride = 1 << level
        active = lane % stride == 0
        second = lane % (2 * stride) == stride
        keep = jnp.where(active, jnp.where(second, -0.5, 0.5), 1.0).astype(jnp.float32)
        swap = jnp.where(active, 0.5, 0.0).astype(jnp.float32)

        def lane_step(values):
            after = each(lambda value: pltpu.roll(value, LANES - stride, 1), values)
            before = each(lambda value: pltpu.roll(value, stride, 1), values)
            return each(
                lambda value, high, low: value * keep + jnp.where(second, low, high) * swap,
                values,
                after,
                before,
            )

        def row_step(first, other):
            if level == 0:
                return each(jnp.add, first, other), each(jnp.subtract, first, other)
            return (
                each(lambda a, b: jnp.where(active, a + b, a), first, other),
                each(lambda a, b: jnp.where(active, a - b, b), first, other),
            )

        return lane_step, row_step

    def shrink(values, kept=None):
        factors = []
        for real, imag in zip(*values):
            power = real * real + imag * imag
            factor = jnp.maximum(
                1.0 - THRESHOLD * lax.rsqrt(jnp.maximum(power, THRESHOLD * THRESHOLD)), 0.0
            )
            factors.append(factor if kept is None else jnp.where(kept, 1.0, factor))
        return [[value * factor for value, factor in zip(row, factors)] for row in values]

    def load(ref, start, stride=None):
        where = pl.ds(start, TILE) if stride is None else pl.ds(start, TILE, stride=stride)
        return [[ref[part, column, where, :] for column in range(columns)] for part in range(2)]

    def save(ref, values, start, stride=None):
        where = pl.ds(start, TILE) if stride is None else pl.ds(start, TILE, stride=stride)
        for part in range(2):
            for column in range(columns):
                ref[part, column, where, :] = values[part][column]

    for level in range(LEVELS - 1):
        lane_step, row_step = level_steps(level)

        for index in range(height >> (level + 4)):
            base = index * 2 * TILE
            first = load(levels[level], base, 2)
            other = load(levels[level], base + 1, 2)
            low, high = row_step(first, other)
            save(levels[level + 1], lane_step(low), index * TILE)
            save(details[level], shrink(lane_step(high)), index * TILE)

    lane_step, row_step = level_steps(LEVELS - 1)
    coarsest = lane % (1 << LEVELS) == 0
    for index in range(height >> (LEVELS + 3)):
        base = index * 2 * TILE
        low, high = row_step(load(levels[-1], base, 2), load(levels[-1], base + 1, 2))
        low = lane_step(shrink(lane_step(low), coarsest))
        high = lane_step(shrink(lane_step(high)))
        first, other = row_step(low, high)
        save(levels[-1], first, base, 2)
        save(levels[-1], other, base + 1, 2)

    for level in range(LEVELS - 1)[::-1]:
        lane_step, row_step = level_steps(level)
        for index in range(height >> (level + 4)):
            low = lane_step(load(levels[level + 1], index * TILE))
            high = lane_step(load(details[level], index * TILE))
            first, other = row_step(low, high)
            base = index * 2 * TILE
            save(levels[level], first, base, 2)
            save(levels[level], other, base + 1, 2)
    for part in range(2):
        for column in range(columns):
            out[part, :, pl.ds(column * LANES, LANES)] = work[part, column]


def shrink_object(place_of, *pieces):
    smem = pl.BlockSpec(memory_space=pltpu.SMEM)
    vmem = pl.BlockSpec(memory_space=pltpu.VMEM)
    shape = pieces[0].shape
    sizes = [(2, shape[2] // LANES, shape[1] >> level, LANES) for level in range(LEVELS)]
    return pl.pallas_call(
        haar_kernel,
        out_shape=jax.ShapeDtypeStruct(shape, jnp.float32),
        in_specs=[smem] * 2 + [vmem] * len(pieces),
        out_specs=vmem,
        scratch_shapes=[pltpu.VMEM(size, jnp.float32) for size in sizes + sizes[1:]],
        compiler_params=pltpu.CompilerParams(vmem_limit_bytes=16 * MIB),
        name="haar",
    )(*place_of, *pieces)


def join_kernel(core_of, first, second, given, kept, first_out, second_out, shares):
    margin = first.shape[1]
    width = first.shape[2]
    near = pl.ds(pl.multiple_of((1 - core_of[0]) * (width - LANES), LANES), LANES)
    first_out[...] = first[...]
    second_out[...] = second[...]
    first_out[:, :, near] += given[:, :margin]
    second_out[:, :, near] += given[:, margin : 2 * margin]
    shares[...] = (kept[...] + given[:, 2 * margin :]).reshape(shares.shape)


def joined(core_of, first, second, given, kept, parts):
    smem = pl.BlockSpec(memory_space=pltpu.SMEM)
    vmem = pl.BlockSpec(memory_space=pltpu.VMEM)
    shapes = [first.shape, second.shape, (parts, kept.size // (parts * LANES), LANES)]
    return pl.pallas_call(
        join_kernel,
        out_shape=tuple(jax.ShapeDtypeStruct(shape, jnp.float32) for shape in shapes),
        in_specs=[smem] + [vmem] * 4,
        out_specs=[vmem] * 3,
        compiler_params=pltpu.CompilerParams(vmem_limit_bytes=8 * MIB),
        name="joined",
    )(core_of, first, second, given, kept)


def added(parts):
    total = parts[0]
    for index in range(1, parts.shape[0]):
        total = total + parts[index]
    return total


def tile_kernel(parts, tile, out):
    scale = PROBE_STEP / (PATCHES * DEVICES)
    out[...] = jnp.broadcast_to((tile[...] - scale * added(parts))[None], out.shape)


def summed(parts, copies, tile):
    vmem = pl.BlockSpec(memory_space=pltpu.VMEM)
    return pl.pallas_call(
        tile_kernel,
        out_shape=jax.ShapeDtypeStruct((copies,) + parts.shape[1:], jnp.float32),
        in_specs=[vmem] * 2,
        out_specs=vmem,
        compiler_params=pltpu.CompilerParams(vmem_limit_bytes=4 * MIB),
        name="summed",
    )(parts, tile)


def probe_kernel(tiles, out):
    rows = tiles.shape[2]
    chunks = out.shape[1] // rows
    for part in range(2):
        for half in range(2):
            value = tiles[pl.ds(part * chunks, chunks), half]
            out[part, :, pl.ds(half * LANES, LANES)] = value.reshape(out.shape[1], LANES)


def laid_out(tiles, shape):
    vmem = pl.BlockSpec(memory_space=pltpu.VMEM)
    return pl.pallas_call(
        probe_kernel,
        out_shape=jax.ShapeDtypeStruct(shape, jnp.float32),
        in_specs=[vmem],
        out_specs=vmem,
        compiler_params=pltpu.CompilerParams(vmem_limit_bytes=4 * MIB),
        name="laid_out",
    )(tiles)


def permuted(value, move):
    rows, cols = lax.axis_size(ROW), lax.axis_size(COL)
    pairs = []
    for source in range(rows * cols):
        row, col = move(source // cols, source % cols)
        if 0 <= row < rows and 0 <= col < cols:
            pairs.append((source, row * cols + col))
    return lax.ppermute(value, AXES, pairs)


def up_by(step):
    return lambda row, col: (row + step, col)


def near_to(row, col):
    return row, col ^ 1


def far_to(step):
    return lambda row, col: (row + step, col - 1 if col % 2 == 0 else col + 1)


def pair_to(first):
    return lambda row, col: (row + (1 if (row % 2 == 0) == first else -1), col)


def on_device(object_now, object_prev, probe, amplitudes, pos_row, pos_col, counts):
    centre = object_now + MOMENTUM * (object_now - object_prev)
    margin = probe.shape[1] // 2
    height, width = centre.shape[1:]
    slots = amplitudes.shape[2]
    core = lax.axis_index("core")
    place_of = core.reshape(1), lax.axis_index("xh").reshape(1)

    def sides(value):
        first, last = value[:, :, :margin], value[:, :, width - margin :]
        return jnp.where(core == 0, last, first), jnp.where(core == 0, first, last)

    near, far = sides(centre)
    top = permuted(centre[:, height - margin :], up_by(1))
    bottom = permuted(centre[:, :margin], up_by(-1))
    far_top = permuted(far[:, height - margin :], far_to(1))
    far_bottom = permuted(far[:, :margin], far_to(-1))
    far_mid = permuted(far, far_to(0))
    near_mid = permuted(near, near_to)
    near_corner, far_top, far_bottom, far_mid = lax.optimization_barrier(
        (
            jnp.concatenate([sides(top)[0], sides(bottom)[0]], axis=1),
            far_top,
            far_bottom,
            far_mid,
        )
    )
    near_corner = permuted(near_corner, near_to)
    (
        inner,
        first,
        second,
        near_mid,
        far_mid,
        given,
        far_top,
        far_bottom,
        probe_kept,
    ) = patches(
        counts.reshape(1),
        pos_row.reshape(slots),
        pos_col.reshape(slots),
        place_of,
        (centre, top, bottom, near_mid, far_mid, near_corner, far_top, far_bottom),
        probe,
        amplitudes[0, 0],
    )
    given = permuted(given, near_to)
    first, second, shares = joined(
        place_of[0], first, second, given, probe_kept, lax.axis_size(CHIPS)
    )
    first, second, far_top, far_bottom, far_mid, near_mid, shares = lax.optimization_barrier(
        (first, second, far_top, far_bottom, far_mid, near_mid, shares)
    )
    first = permuted(first, pair_to(True))
    first, second = lax.optimization_barrier((first, second))
    second = permuted(second, pair_to(False))
    far_below = permuted(far_top, far_to(-1))
    far_above = permuted(far_bottom, far_to(1))
    far_mid, far_below, far_above = lax.optimization_barrier((far_mid, far_below, far_above))
    far_mid = permuted(far_mid, far_to(0))
    near_mid, first, second, far_mid = lax.optimization_barrier(
        (near_mid, first, second, far_mid)
    )
    near_mid = permuted(near_mid, near_to)
    shares = lax.all_to_all(shares, CHIPS, 0, 0, tiled=True)
    columns = [probe[:, :, LANES * index : LANES * (index + 1)] for index in range(2)]
    tile = jnp.where(core == 0, *columns).reshape(shares.shape)
    tile = lax.dynamic_index_in_dim(tile, lax.axis_index(CHIPS), keepdims=False)
    tiles = summed(shares, lax.axis_size(AXES), tile)
    tiles = lax.all_to_all(tiles, AXES, 0, 0, tiled=True)
    object_new = shrink_object(
        place_of, inner, first, second, near_mid, far_mid, far_above, far_below
    )
    object_new, tiles = lax.optimization_barrier((object_new, tiles))
    probe_new = laid_out(tiles.reshape((-1, 2) + tile.shape), probe.shape)
    return object_new, probe_new


def solution(mesh):
    fine = jax.sharding.Mesh(mesh.devices.reshape(4, 2, 4, 2, 2), AXES)
    in_specs = (
        P(None, ROW, COL),
        P(None, ROW, COL),
        P(),
        P(ROW, COL, None, None, None),
        P(ROW, COL, None),
        P(ROW, COL, None),
        P(ROW, COL),
    )
    out_specs = (P(None, ROW, COL), P())
    return jax.shard_map(
        on_device, mesh=fine, in_specs=in_specs, out_specs=out_specs, check_vma=False
    )
```

```python
import math

import jax
import jax.numpy as jnp
import ml_dtypes
import numpy as np
from jax import lax
from jax.experimental import pallas as pl
from jax.experimental.pallas import tpu as pltpu
from jax.sharding import PartitionSpec as P

LEVELS = 4
MOMENTUM = 0.6
STEP_OBJECT = 0.5
PROBE_STEP = 2.0
THRESHOLD = 0.3
FLOOR = 0.5

ROW = ("z", "xh")
COL = ("y", "xl", "core")
AXES = ROW + COL
CHIPS = ROW + COL[:2]
LANES = 128
PATCHES = 4
DEVICES = 128
TILE = 8
MIB = 1024 * 1024


def split_table(table):
    high = table.astype(ml_dtypes.bfloat16)
    low = (table - high.astype(np.float64)).astype(ml_dtypes.bfloat16)
    return high, low


def dft_tables(length):
    half = length // 2
    points = np.arange(half)
    angles = (points[:, None] * points[None, :] % half) * (-2.0 * math.pi / half)
    real = np.cos(angles) / math.sqrt(length)
    imag = np.sin(angles) / math.sqrt(length)
    left_high, left_low = split_table(np.block([[real, -imag], [imag, real]]))
    right_high, right_low = split_table(np.block([[real, imag], [-imag, real]]))
    turn = points * (-2.0 * math.pi / length)
    twiddle = np.stack([np.cos(turn), np.sin(turn)]).astype(np.float32)
    return (
        np.concatenate([left_high, left_high, left_low], axis=1),
        np.concatenate([right_high, right_high, right_low], axis=0),
        np.concatenate(
            [np.repeat(twiddle[:, :, None], LANES, axis=2), np.repeat(twiddle[:, None, :], half, axis=1)]
        ),
    )


def split_value(value):
    high = value.astype(jnp.bfloat16)
    low = (value - high.astype(jnp.float32)).astype(jnp.bfloat16)
    return high, low


def times(real, imag, twiddle):
    cosine, sine = twiddle
    return real * cosine - imag * sine, real * sine + imag * cosine


def left_product(blocks, table):
    half = blocks[0][0].shape[0]
    width = blocks[0][0].shape[1]
    value = jnp.concatenate(
        [jnp.concatenate([real, imag], axis=0) for real, imag in blocks], axis=1
    )
    high, low = split_value(value)
    out = jnp.dot(
        table[...],
        jnp.concatenate([high, low, high], axis=0),
        preferred_element_type=jnp.float32,
    )
    return [
        (out[:half, index * width : (index + 1) * width], out[half:, index * width : (index + 1) * width])
        for index in range(len(blocks))
    ]


def right_product(blocks, table):
    half = blocks[0][0].shape[1]
    value = jnp.concatenate(
        [jnp.concatenate([real, imag], axis=1) for real, imag in blocks], axis=0
    )
    high, low = split_value(value)
    out = jnp.dot(
        jnp.concatenate([high, low, high], axis=1),
        table[...],
        preferred_element_type=jnp.float32,
    )
    return [
        (out[index * half : (index + 1) * half, :half], out[index * half : (index + 1) * half, half:])
        for index in range(len(blocks))
    ]


def forward(real, imag, left_table, right_table, row_twiddle, lane_twiddle):
    half = real.shape[0] // 2
    wide_twiddle = [jnp.concatenate([part, part], axis=1) for part in row_twiddle]
    total = (real[:half] + real[half:], imag[:half] + imag[half:])
    gap = times(real[:half] - real[half:], imag[:half] - imag[half:], wide_twiddle)
    blocks = []
    for real, imag in left_product([total, gap], left_table):
        blocks.append((real[:, :half] + real[:, half:], imag[:, :half] + imag[:, half:]))
        blocks.append(
            times(real[:, :half] - real[:, half:], imag[:, :half] - imag[:, half:], lane_twiddle)
        )
    return right_product(blocks, right_table)


def backward(blocks, left_table, right_table, row_twiddle, lane_twiddle):
    blocks = right_product(blocks, right_table)
    wide_twiddle = [jnp.concatenate([part, part], axis=1) for part in row_twiddle]
    joined = []
    for parity in range(2):
        even_real, even_imag = blocks[2 * parity]
        odd_real, odd_imag = times(*blocks[2 * parity + 1], lane_twiddle)
        joined.append(
            (
                jnp.concatenate([even_real + odd_real, even_real - odd_real], axis=1),
                jnp.concatenate([even_imag + odd_imag, even_imag - odd_imag], axis=1),
            )
        )
    (even_real, even_imag), odd = left_product(joined, left_table)
    odd_real, odd_imag = times(*odd, wide_twiddle)
    return (
        jnp.concatenate([even_real + odd_real, even_real - odd_real], axis=0),
        jnp.concatenate([even_imag + odd_imag, even_imag - odd_imag], axis=0),
    )


def amplitude_kernel(amplitude, table, out, sorted_lanes):
    slots, size, _ = amplitude.shape
    half = size // 2
    for slot in range(slots):
        value = amplitude[slot]
        high = value.astype(jnp.bfloat16)
        rest = value - high.astype(jnp.float32)
        middle, low = split_value(rest)
        ordered = jnp.dot(
            jnp.concatenate([high, middle, low], axis=1),
            table[...],
            preferred_element_type=jnp.float32,
        )
        for index in range(2):
            sorted_lanes[slot, index] = ordered[:, index * half : (index + 1) * half]
            for parity in range(2):
                out[slot, 2 * parity + index] = sorted_lanes[slot, index, pl.ds(parity, half, stride=2), :]


def ordered_amplitude(amplitude):
    slots, size, _ = amplitude.shape
    half = size // 2
    table = np.zeros((size, size), np.float32)
    table[2 * np.arange(half), np.arange(half)] = 1
    table[2 * np.arange(half) + 1, half + np.arange(half)] = 1
    table = np.concatenate([table] * 3, axis=0).astype(ml_dtypes.bfloat16)
    vmem = pl.BlockSpec(memory_space=pltpu.VMEM)
    return pl.pallas_call(
        amplitude_kernel,
        out_shape=jax.ShapeDtypeStruct((slots, 4, half, half), jnp.float32),
        in_specs=[vmem, vmem],
        out_specs=vmem,
        scratch_shapes=[pltpu.VMEM((slots, 2, size, half), jnp.float32)],
        compiler_params=pltpu.CompilerParams(vmem_limit_bytes=8 * MIB),
        cost_estimate=pl.CostEstimate(
            flops=2 * slots * size**3 * 3, bytes_accessed=8 * slots * size**2, transcendentals=0
        ),
        name="ordered_amplitude",
    )(amplitude, jnp.asarray(table))


def patch_kernel(
    counts,
    rows,
    cols,
    core_of,
    odd_of,
    centre,
    top,
    bottom,
    near_mid,
    far_mid,
    near_corner,
    far_top,
    far_bottom,
    probe,
    amplitude,
    left_table,
    right_table,
    twiddle_table,
    inner_out,
    first_out,
    second_out,
    near_mid_out,
    far_mid_out,
    given_out,
    far_top_out,
    far_bottom_out,
    probe_out,
    extended,
    gradient,
    probe_sum,
    sems,
):
    size = probe.shape[1]
    margin = size // 2
    height, width = centre.shape[1:]
    inner = pl.ds(margin, width)
    core, odd = core_of[0], odd_of[0]
    near = pl.ds(pl.multiple_of((1 - core) * (margin + width), LANES), margin)
    far = pl.ds(pl.multiple_of(core * (margin + width), LANES), margin)
    first = pl.ds(pl.multiple_of((1 - odd) * (margin + height), margin), margin)
    second = pl.ds(pl.multiple_of(odd * (margin + height), margin), margin)
    head, middle, tail = pl.ds(0, margin), pl.ds(margin, height), pl.ds(margin + height, margin)
    moves = [
        (centre, extended.at[:, middle, inner]),
        (near_mid, extended.at[:, middle, near]),
        (far_mid, extended.at[:, middle, far]),
        (top, extended.at[:, head, inner]),
        (bottom, extended.at[:, tail, inner]),
        (far_top, extended.at[:, head, far]),
        (far_bottom, extended.at[:, tail, far]),
        (near_corner.at[:, head, :], extended.at[:, head, near]),
        (near_corner.at[:, pl.ds(margin, margin), :], extended.at[:, tail, near]),
    ]
    copies = [
        pltpu.make_async_copy(source, target, sems.at[index])
        for index, (source, target) in enumerate(moves)
    ]
    for copy in copies:
        copy.start()
    gradient[...] = jnp.zeros_like(gradient)
    probe_sum[...] = jnp.zeros_like(probe_sum)
    for copy in copies:
        copy.wait()
    tile = (1, TILE, LANES)
    lane = lax.broadcasted_iota(jnp.int32, tile, 2)
    sublane = lax.broadcasted_iota(jnp.int32, tile, 1)
    tiles = size // TILE
    pieces = size // LANES

    tables = (
        left_table,
        right_table,
        (twiddle_table[0], twiddle_table[1]),
        (twiddle_table[2], twiddle_table[3]),
    )

    def place(slot):
        row_shift = lax.rem(rows[slot], TILE)
        col_shift = lax.rem(cols[slot], LANES)
        row = pl.multiple_of(rows[slot] - row_shift, TILE)
        col = pl.multiple_of(cols[slot] - col_shift, LANES)
        areas = [
            (pl.ds(row, size + TILE), pl.ds(col + LANES * piece, LANES))
            for piece in range(pieces + 1)
        ]
        return row_shift, col_shift, areas

    def window(part, row_shift, col_shift, areas):
        columns = [
            pltpu.roll(
                extended[(part,) + area].reshape(tiles + 1, TILE, LANES),
                lax.rem(LANES - col_shift, LANES),
                2,
            )
            for area in areas
        ]
        result = []
        for piece in range(pieces):
            value = jnp.where(lane < LANES - col_shift, columns[piece], columns[piece + 1])
            value = pltpu.roll(value, lax.rem(TILE - row_shift, TILE), 1)
            value = jnp.where(sublane < TILE - row_shift, value[:tiles], value[1:])
            result.append(value.reshape(size, LANES))
        return jnp.concatenate(result, axis=1)

    def add_term(part, term, row_shift, col_shift, areas):
        columns = []
        ended = jnp.zeros(tile, jnp.float32)
        for piece in range(pieces):
            value = term[:, LANES * piece : LANES * (piece + 1)].reshape(tiles, TILE, LANES)
            value = pltpu.roll(value, row_shift, 1)
            value = jnp.where(
                sublane >= row_shift,
                jnp.concatenate([value, ended], axis=0),
                jnp.concatenate([ended, value], axis=0),
            )
            columns.append(pltpu.roll(value, col_shift, 2))
        ended = jnp.zeros_like(columns[0])
        columns = [ended] + columns + [ended]
        for piece, area in enumerate(areas):
            block = jnp.where(lane >= col_shift, columns[piece + 1], columns[piece])
            gradient[(part,) + area] += block.reshape(size + TILE, LANES)

    def some_patches(slots):
        places = [place(slot) for slot in slots]
        windows = [[window(part, *where) for part in range(2)] for where in places]
        probe_real = probe[0]
        probe_imag = probe[1]
        far_fields = [
            forward(
                probe_real * real - probe_imag * imag, probe_real * imag + probe_imag * real, *tables
            )
            for real, imag in windows
        ]
        residuals = []
        for slot, far_field in zip(slots, far_fields):
            residual = []
            for index, (real, imag) in enumerate(far_field):
                power = real * real + imag * imag
                remain = 1.0 - amplitude[slot, index] * lax.rsqrt(
                    jnp.maximum(power, FLOOR * FLOOR)
                )
                residual.append((real * remain, -imag * remain))
            residuals.append(residual)
        backs = [backward(residual, *tables) for residual in residuals]
        probe_terms = [0.0, 0.0]
        for where, (window_real, window_imag), (back_real, back_imag) in zip(places, windows, backs):
            back_imag = -back_imag
            probe_terms[0] += window_real * back_real + window_imag * back_imag
            probe_terms[1] += window_real * back_imag - window_imag * back_real
            add_term(0, probe_real * back_real + probe_imag * back_imag, *where)
            add_term(1, probe_real * back_imag - probe_imag * back_real, *where)
        for part, term in enumerate(probe_terms):
            for piece in range(pieces):
                probe_sum[part, piece] += term[:, LANES * piece : LANES * (piece + 1)]

    def two_patches(index, carry):
        some_patches([2 * index, 2 * index + 1])
        return carry

    count = counts[0]
    lax.fori_loop(0, count // 2, two_patches, 0)

    @pl.when(count % 2 == 1)
    def _():
        some_patches([count - 1])

    gradient[:, middle, inner] = (
        extended[:, middle, inner] - STEP_OBJECT * gradient[:, middle, inner]
    )
    inner_copy = pltpu.make_async_copy(gradient.at[:, middle, inner], inner_out, sems.at[0])
    inner_copy.start()
    given_out[:, :margin] = gradient[:, first, near]
    given_out[:, margin : 2 * margin] = gradient[:, second, near]
    for part in range(2):
        given_out[part, 2 * margin :] = probe_sum[part, 1 - core]
        probe_out[part] = probe_sum[part, core]
    first_out[...] = gradient[:, first, inner]
    second_out[...] = gradient[:, second, inner]
    near_mid_out[...] = gradient[:, middle, near]
    far_mid_out[...] = gradient[:, middle, far]
    far_top_out[...] = gradient[:, head, far]
    far_bottom_out[...] = gradient[:, tail, far]
    inner_copy.wait()


def patches(counts, rows, cols, place_of, pieces, probe, amplitude):
    size = probe.shape[1]
    margin = size // 2
    height, width = pieces[0].shape[1:]
    tall, wide = height + size, width + size
    smem = pl.BlockSpec(memory_space=pltpu.SMEM)
    vmem = pl.BlockSpec(memory_space=pltpu.VMEM)
    anywhere = pl.BlockSpec(memory_space=pl.ANY)
    shapes = [
        (height, width),
        (margin, width),
        (margin, width),
        (height, margin),
        (height, margin),
        (2 * margin + size, margin),
        (margin, margin),
        (margin, margin),
        (size, LANES),
    ]
    return pl.pallas_call(
        patch_kernel,
        out_shape=(pltpu.HBM((2,) + shapes[0], jnp.float32),)
        + tuple(jax.ShapeDtypeStruct((2,) + shape, jnp.float32) for shape in shapes[1:]),
        in_specs=[smem] * 5 + [anywhere] * 8 + [vmem] * 5,
        out_specs=[anywhere] + [vmem] * 8,
        scratch_shapes=[
            pltpu.VMEM((2, tall, wide), jnp.float32),
            pltpu.VMEM((2, tall, wide), jnp.float32),
            pltpu.VMEM((2, size // LANES, size, LANES), jnp.float32),
            pltpu.SemaphoreType.DMA((9,)),
        ],
        compiler_params=pltpu.CompilerParams(vmem_limit_bytes=28 * MIB),
        name="patches",
    )(
        counts,
        rows,
        cols,
        *place_of,
        *pieces,
        probe,
        amplitude,
        *(jnp.asarray(table) for table in dft_tables(size)),
    )


def haar_kernel(
    core_of,
    odd_of,
    inner,
    first,
    second,
    near_mid,
    far_mid,
    far_top,
    far_bottom,
    out,
    *scratch,
):
    height, width = inner.shape[1:]
    margin = first.shape[1]
    core, odd = core_of[0], odd_of[0]
    levels = [scratch[level] for level in range(LEVELS)]
    details = [scratch[LEVELS + level] for level in range(LEVELS - 1)]
    columns = width // LANES
    work = levels[0]
    near = (1 - core) * (columns - 1)
    far = core * (columns - 1)
    first_rows = pl.ds(pl.multiple_of((1 - odd) * (height - margin), margin), margin)
    second_rows = pl.ds(pl.multiple_of(odd * (height - margin), margin), margin)
    for part in range(2):
        for column in range(columns):
            piece = part, slice(None), pl.ds(column * LANES, LANES)
            work[part, column] = inner[piece]
            work[part, column, first_rows] -= STEP_OBJECT * first[piece]
            work[part, column, second_rows] -= STEP_OBJECT * second[piece]
        work[part, near] -= STEP_OBJECT * near_mid[part]
        corners = jnp.concatenate([far_top[part], far_bottom[part]], axis=0)
        work[part, far] -= STEP_OBJECT * (far_mid[part] + corners)

    lane = lax.broadcasted_iota(jnp.int32, (TILE, LANES), 1)

    def each(function, *parts):
        return [[function(*pair) for pair in zip(*rows)] for rows in zip(*parts)]

    def level_steps(level):
        stride = 1 << level
        active = lane % stride == 0
        second = lane % (2 * stride) == stride
        keep = jnp.where(active, jnp.where(second, -0.5, 0.5), 1.0).astype(jnp.float32)
        swap = jnp.where(active, 0.5, 0.0).astype(jnp.float32)

        def lane_step(values):
            after = each(lambda value: pltpu.roll(value, LANES - stride, 1), values)
            before = each(lambda value: pltpu.roll(value, stride, 1), values)
            return each(
                lambda value, high, low: value * keep + jnp.where(second, low, high) * swap,
                values,
                after,
                before,
            )

        def row_step(first, other):
            if level == 0:
                return each(jnp.add, first, other), each(jnp.subtract, first, other)
            return (
                each(lambda a, b: jnp.where(active, a + b, a), first, other),
                each(lambda a, b: jnp.where(active, a - b, b), first, other),
            )

        return lane_step, row_step

    def shrink(values, kept=None):
        factors = []
        for real, imag in zip(*values):
            power = real * real + imag * imag
            factor = jnp.maximum(
                1.0 - THRESHOLD * lax.rsqrt(jnp.maximum(power, THRESHOLD * THRESHOLD)), 0.0
            )
            factors.append(factor if kept is None else jnp.where(kept, 1.0, factor))
        return [[value * factor for value, factor in zip(row, factors)] for row in values]

    def load(ref, start, stride=None):
        where = pl.ds(start, TILE) if stride is None else pl.ds(start, TILE, stride=stride)
        return [[ref[part, column, where, :] for column in range(columns)] for part in range(2)]

    def save(ref, values, start, stride=None):
        where = pl.ds(start, TILE) if stride is None else pl.ds(start, TILE, stride=stride)
        for part in range(2):
            for column in range(columns):
                ref[part, column, where, :] = values[part][column]

    for level in range(LEVELS - 1):
        lane_step, row_step = level_steps(level)

        for index in range(height >> (level + 4)):
            base = index * 2 * TILE
            first = load(levels[level], base, 2)
            other = load(levels[level], base + 1, 2)
            low, high = row_step(first, other)
            save(levels[level + 1], lane_step(low), index * TILE)
            save(details[level], shrink(lane_step(high)), index * TILE)

    lane_step, row_step = level_steps(LEVELS - 1)
    coarsest = lane % (1 << LEVELS) == 0
    for index in range(height >> (LEVELS + 3)):
        base = index * 2 * TILE
        low, high = row_step(load(levels[-1], base, 2), load(levels[-1], base + 1, 2))
        low = lane_step(shrink(lane_step(low), coarsest))
        high = lane_step(shrink(lane_step(high)))
        first, other = row_step(low, high)
        save(levels[-1], first, base, 2)
        save(levels[-1], other, base + 1, 2)

    for level in range(LEVELS - 1)[::-1]:
        lane_step, row_step = level_steps(level)
        for index in range(height >> (level + 4)):
            low = lane_step(load(levels[level + 1], index * TILE))
            high = lane_step(load(details[level], index * TILE))
            first, other = row_step(low, high)
            base = index * 2 * TILE
            save(levels[level], first, base, 2)
            save(levels[level], other, base + 1, 2)
    for part in range(2):
        for column in range(columns):
            out[part, :, pl.ds(column * LANES, LANES)] = work[part, column]


def shrink_object(place_of, *pieces):
    smem = pl.BlockSpec(memory_space=pltpu.SMEM)
    vmem = pl.BlockSpec(memory_space=pltpu.VMEM)
    shape = pieces[0].shape
    sizes = [(2, shape[2] // LANES, shape[1] >> level, LANES) for level in range(LEVELS)]
    return pl.pallas_call(
        haar_kernel,
        out_shape=jax.ShapeDtypeStruct(shape, jnp.float32),
        in_specs=[smem] * 2 + [vmem] * len(pieces),
        out_specs=vmem,
        scratch_shapes=[pltpu.VMEM(size, jnp.float32) for size in sizes + sizes[1:]],
        compiler_params=pltpu.CompilerParams(vmem_limit_bytes=16 * MIB),
        name="haar",
    )(*place_of, *pieces)


def join_kernel(core_of, first, second, given, kept, first_out, second_out, shares):
    margin = first.shape[1]
    width = first.shape[2]
    near = pl.ds(pl.multiple_of((1 - core_of[0]) * (width - LANES), LANES), LANES)
    first_out[...] = first[...]
    second_out[...] = second[...]
    first_out[:, :, near] += given[:, :margin]
    second_out[:, :, near] += given[:, margin : 2 * margin]
    shares[...] = (kept[...] + given[:, 2 * margin :]).reshape(shares.shape)


def joined(core_of, first, second, given, kept, parts):
    smem = pl.BlockSpec(memory_space=pltpu.SMEM)
    vmem = pl.BlockSpec(memory_space=pltpu.VMEM)
    shapes = [first.shape, second.shape, (parts, kept.size // (parts * LANES), LANES)]
    return pl.pallas_call(
        join_kernel,
        out_shape=tuple(jax.ShapeDtypeStruct(shape, jnp.float32) for shape in shapes),
        in_specs=[smem] + [vmem] * 4,
        out_specs=[vmem] * 3,
        compiler_params=pltpu.CompilerParams(vmem_limit_bytes=8 * MIB),
        name="joined",
    )(core_of, first, second, given, kept)


def added(parts):
    total = parts[0]
    for index in range(1, parts.shape[0]):
        total = total + parts[index]
    return total


def tile_kernel(parts, tile, out):
    scale = PROBE_STEP / (PATCHES * DEVICES)
    out[...] = jnp.broadcast_to((tile[...] - scale * added(parts))[None], out.shape)


def summed(parts, copies, tile):
    vmem = pl.BlockSpec(memory_space=pltpu.VMEM)
    return pl.pallas_call(
        tile_kernel,
        out_shape=jax.ShapeDtypeStruct((copies,) + parts.shape[1:], jnp.float32),
        in_specs=[vmem] * 2,
        out_specs=vmem,
        compiler_params=pltpu.CompilerParams(vmem_limit_bytes=4 * MIB),
        name="summed",
    )(parts, tile)


def probe_kernel(tiles, out):
    rows = tiles.shape[2]
    chunks = out.shape[1] // rows
    for part in range(2):
        for half in range(2):
            value = tiles[pl.ds(part * chunks, chunks), half]
            out[part, :, pl.ds(half * LANES, LANES)] = value.reshape(out.shape[1], LANES)


def laid_out(tiles, shape):
    vmem = pl.BlockSpec(memory_space=pltpu.VMEM)
    return pl.pallas_call(
        probe_kernel,
        out_shape=jax.ShapeDtypeStruct(shape, jnp.float32),
        in_specs=[vmem],
        out_specs=vmem,
        compiler_params=pltpu.CompilerParams(vmem_limit_bytes=4 * MIB),
        name="laid_out",
    )(tiles)


def permuted(value, move):
    rows, cols = lax.axis_size(ROW), lax.axis_size(COL)
    pairs = []
    for source in range(rows * cols):
        row, col = move(source // cols, source % cols)
        if 0 <= row < rows and 0 <= col < cols:
            pairs.append((source, row * cols + col))
    return lax.ppermute(value, AXES, pairs)


def up_by(step):
    return lambda row, col: (row + step, col)


def near_to(row, col):
    return row, col ^ 1


def far_to(step):
    return lambda row, col: (row + step, col - 1 if col % 2 == 0 else col + 1)


def pair_to(first):
    return lambda row, col: (row + (1 if (row % 2 == 0) == first else -1), col)


def on_device(object_now, object_prev, probe, amplitudes, pos_row, pos_col, counts):
    centre = object_now + MOMENTUM * (object_now - object_prev)
    margin = probe.shape[1] // 2
    height, width = centre.shape[1:]
    slots = amplitudes.shape[2]
    core = lax.axis_index("core")
    place_of = core.reshape(1), lax.axis_index("xh").reshape(1)

    def sides(value):
        first, last = value[:, :, :margin], value[:, :, width - margin :]
        return jnp.where(core == 0, last, first), jnp.where(core == 0, first, last)

    near, far = sides(centre)
    top = permuted(centre[:, height - margin :], up_by(1))
    bottom = permuted(centre[:, :margin], up_by(-1))
    far_top = permuted(far[:, height - margin :], far_to(1))
    far_bottom = permuted(far[:, :margin], far_to(-1))
    far_mid = permuted(far, far_to(0))
    near_mid = permuted(near, near_to)
    near_corner, far_top, far_bottom, far_mid = lax.optimization_barrier(
        (
            jnp.concatenate([sides(top)[0], sides(bottom)[0]], axis=1),
            far_top,
            far_bottom,
            far_mid,
        )
    )
    near_corner = permuted(near_corner, near_to)
    (
        inner,
        first,
        second,
        near_mid,
        far_mid,
        given,
        far_top,
        far_bottom,
        probe_kept,
    ) = patches(
        counts.reshape(1),
        pos_row.reshape(slots),
        pos_col.reshape(slots),
        place_of,
        (centre, top, bottom, near_mid, far_mid, near_corner, far_top, far_bottom),
        probe,
        ordered_amplitude(amplitudes[0, 0]),
    )
    given = permuted(given, near_to)
    first, second, shares = joined(
        place_of[0], first, second, given, probe_kept, lax.axis_size(CHIPS)
    )
    first, second, far_top, far_bottom, far_mid, near_mid, shares = lax.optimization_barrier(
        (first, second, far_top, far_bottom, far_mid, near_mid, shares)
    )
    first = permuted(first, pair_to(True))
    first, second = lax.optimization_barrier((first, second))
    second = permuted(second, pair_to(False))
    far_below = permuted(far_top, far_to(-1))
    far_above = permuted(far_bottom, far_to(1))
    far_mid, far_below, far_above = lax.optimization_barrier((far_mid, far_below, far_above))
    far_mid = permuted(far_mid, far_to(0))
    near_mid, first, second, far_mid = lax.optimization_barrier(
        (near_mid, first, second, far_mid)
    )
    near_mid = permuted(near_mid, near_to)
    shares = lax.all_to_all(shares, CHIPS, 0, 0, tiled=True)
    columns = [probe[:, :, LANES * index : LANES * (index + 1)] for index in range(2)]
    tile = jnp.where(core == 0, *columns).reshape(shares.shape)
    tile = lax.dynamic_index_in_dim(tile, lax.axis_index(CHIPS), keepdims=False)
    tiles = summed(shares, lax.axis_size(AXES), tile)
    tiles = lax.all_to_all(tiles, AXES, 0, 0, tiled=True)
    object_new = shrink_object(
        place_of, inner, first, second, near_mid, far_mid, far_above, far_below
    )
    object_new, tiles = lax.optimization_barrier((object_new, tiles))
    probe_new = laid_out(tiles.reshape((-1, 2) + tile.shape), probe.shape)
    return object_new, probe_new


def solution(mesh):
    fine = jax.sharding.Mesh(mesh.devices.reshape(4, 2, 4, 2, 2), AXES)
    in_specs = (
        P(None, ROW, COL),
        P(None, ROW, COL),
        P(),
        P(ROW, COL, None, None, None),
        P(ROW, COL, None),
        P(ROW, COL, None),
        P(ROW, COL),
    )
    out_specs = (P(None, ROW, COL), P())
    return jax.shard_map(
        on_device, mesh=fine, in_specs=in_specs, out_specs=out_specs, check_vma=False
    )
```
